32 devices in a mesh: group: 2 (over y), tensor: 16 (over z, x, core).
Axes of the slice: x: 2, y: 2, z: 4, core: 2. Of those that a mesh axis runs over, the one named last changes fastest.
Arguments:
- x_coded: bfloat16 [256, 16384], P('group', 'tensor'), parts along dimension 0, may hold values from -1 to 1
- x_scales: bfloat16 [128, 256], P('tensor', 'group'), parts along dimension 1, may hold values from 0.29882812 to 3
- signs: int32 [16384], replicated, may hold values from 0 to 1
- block_order: int32 [32], P('group'), parts along dimension 0, may hold values from 0 to 15, each once
- norm_gain: bfloat16 [16384], replicated, may hold values from 0.099609375 to 1.8984375
- w_query: bfloat16 [16384, 2048], P(None, 'tensor'), may hold values from -0.046875 to 0.046875
- w_key: bfloat16 [16384, 1024], P('tensor'), may hold values from -0.046875 to 0.046875
- w_value: bfloat16 [16384, 1024], P('tensor'), may hold values from -0.046875 to 0.046875
- w_out: bfloat16 [2048, 16384], P('tensor'), may hold values from -0.125 to 0.125
Outputs:
- out_coded: bfloat16 [256, 16384], P('group', 'tensor'), parts along dimension 0
- out_scales: bfloat16 [128, 256], P('tensor', 'group'), parts along dimension 1
The draws below stay inside these ranges and needn't reach their ends.
There are 2 independent parts, one for each index of `group`. The reference program is written for one: setup_inputs(seed, part) draws one part's arguments, and reference() takes and returns one part's arrays. A program takes and returns all parts, laid end to end along the dimension named above; an argument that names none is the same for every part. Nothing has to cross between parts.
Inputs may be any that keep to these rules, and one draw needn't show every extreme that they name: `block_order`: each number 0 to 15 appears once.
All inputs are finite; a program needn't handle non-finite values. Where the reference program divides by a largest or mean magnitude, that divisor is 1e-20 or more.
Results may differ from the reference program's by a relative error of at most 0.011.
Values may be sent and summed in bfloat16 or wider, within the bound.
No kernel may reach another device: no remote copies, remote signals or barrier semaphores. Data moves between devices by JAX's collectives and lax.ppermute only.
A program may use at most 128 MiB of HBM per device.

```python
import math
import jax
import jax.numpy as jnp
from jax import lax

D = 16384
HD = 128
KVH = 8
HEAD_DEV = 1
HEADS = 16
BLK = 128
NBD = 128
TOKENS = 128
NBLOCK = 16
BL = 8
N_TENSOR = 16


def touch_ends(array, own_key, low, high):
    shape = array.shape
    place = [jax.random.randint(jax.random.fold_in(own_key, axis), (), 0, shape[axis]) for axis in range(len(shape))]
    array = array.at[tuple(place)].set(low)
    longest = shape.index(max(shape))
    place[longest] = (place[longest] + 1) % shape[longest]
    return array.at[tuple(place)].set(high)


def levels(rng, dims, cuts, low, top_value):
    level = 1.0
    for axis_at, shards_of in cuts:
        steps = jax.random.uniform(jax.random.fold_in(jax.random.fold_in(rng, 6), axis_at), (shards_of,), jnp.float32, low / len(cuts), top_value / len(cuts))
        level = level * jnp.repeat(jnp.exp(steps), dims[axis_at] // shards_of).reshape((-1,) + (1,) * (len(dims) - 1 - axis_at))
    return level


def centred(key, shape, spread, limit, cuts=(), held_as=jnp.bfloat16):
    loudness = levels(key, shape, cuts, -0.22, 0.18) if cuts else 1.0
    result = jax.random.normal(key, shape, jnp.float32) * spread * loudness
    return jnp.minimum(jnp.maximum(result, -limit), limit).astype(held_as)


def setup_inputs(seed: int = 0, part: int = 0) -> dict:
    key_list = jax.random.split(jax.random.key(seed), 10)
    part_keys = jax.random.split(jax.random.fold_in(key_list[9], part), 10)
    x_coded = jnp.clip(jax.random.uniform(part_keys[0], (TOKENS, D), jnp.float32, -1.0, 1.0) * levels(part_keys[0], (TOKENS, D), ((1, 16),), -0.4, 0.0), -1.0, 1.0).astype(jnp.bfloat16)
    x_scales = jnp.clip(jnp.exp(math.log(3.0) - 2.306499 * jax.random.uniform(part_keys[1], (NBD, TOKENS), jnp.float32) ** levels(part_keys[1], (NBD, TOKENS), ((0, 16),), -0.2, 0.2)), 0.29882812, 3.0).astype(jnp.bfloat16)
    signs = touch_ends(jax.random.randint(key_list[2], (D,), 0, 2), jax.random.fold_in(key_list[2], 1), 0, 1).astype(jnp.int32)
    block_order = jax.random.permutation(part_keys[3], NBLOCK).astype(jnp.int32)
    norm_gain = jnp.clip(1.0 + 0.18 * jax.random.normal(key_list[4], (D,), jnp.float32), 0.099609375, 1.8984375).astype(jnp.bfloat16)
    w_query = centred(key_list[5], (D, HEADS * HD), D ** -0.5, 0.046875, ((1, 16),))
    w_key = centred(key_list[6], (D, KVH * HD), D ** -0.5, 0.046875, ((0, 16),))
    w_value = centred(key_list[7], (D, KVH * HD), D ** -0.5, 0.046875, ((0, 16),))
    w_out = centred(key_list[8], (HEADS * HD, D), (HEADS * HD) ** -0.5, 0.125, ((0, 16),))
    return {"x_coded": x_coded, "x_scales": x_scales, "signs": signs, "block_order": block_order, "norm_gain": norm_gain, "w_query": w_query, "w_key": w_key, "w_value": w_value, "w_out": w_out}


HIGH = lax.Precision.HIGHEST

def hadamard(width):
    idx = jnp.arange(width)
    parity = jnp.zeros((width, width), jnp.int32)
    bit = 1
    while bit < width:
        parity = parity + idx[:, None] // bit % 2 * (idx[None, :] // bit % 2)
        bit = bit * 2
    return jnp.where(parity % 2 == 0, 1.0, -1.0).astype(jnp.float32) / jnp.sqrt(jnp.float32(width))

def rotate_rows(value, sgn, mat):
    rows = value.shape[0]
    blocks = (value * sgn).reshape(rows, -1, mat.shape[0])
    return jnp.einsum('tnb,bc->tnc', blocks, mat, precision=HIGH).reshape(rows, -1)

def unrotate_rows(value, sgn, mat):
    rows = value.shape[0]
    blocks = value.reshape(rows, -1, mat.shape[0])
    return jnp.einsum('tnb,bc->tnc', blocks, mat, precision=HIGH).reshape(rows, -1) * sgn

def encode(rotated, width):
    blocks = rotated.reshape(rotated.shape[0], -1, width)
    scale = (lax.optimization_barrier(jnp.max(jnp.abs(blocks), axis=2)) + 1e-06).astype(jnp.bfloat16)
    coded = (blocks / scale.astype(jnp.float32)[:, :, None]).astype(jnp.bfloat16)
    return (coded.reshape(rotated.shape[0], -1), scale)

def rope(value, positions, heads):
    rows = value.shape[0]
    half = HD // 2
    freqs = 500000.0 ** (-(jnp.arange(half).astype(jnp.float32) * 2.0) / HD)
    angle = positions.astype(jnp.float32)[:, None] * freqs[None, :]
    cosine = jnp.cos(angle)[:, None, :]
    sine = jnp.sin(angle)[:, None, :]
    parts = value.reshape(rows, heads, HD)
    first = parts[:, :, :half]
    second = parts[:, :, half:]
    out = jnp.concatenate([first * cosine - second * sine, second * cosine + first * sine], axis=2)
    return out.reshape(rows, heads * HD)

def reference(x_coded, x_scales, signs, block_order, norm_gain, w_query, w_key, w_value, w_out):
    mat = hadamard(BLK)
    sgn = (2 * signs - 1).astype(jnp.float32)
    deq = x_coded.astype(jnp.float32).reshape(TOKENS, NBD, BLK) * x_scales.astype(jnp.float32).T[:, :, None]
    resid = unrotate_rows(deq.reshape(TOKENS, D), sgn, mat)
    inv = lax.rsqrt(lax.optimization_barrier(jnp.mean(resid * resid, axis=1, keepdims=True)) + 1e-05)
    normed = (resid * norm_gain.astype(jnp.float32) * inv).astype(jnp.bfloat16)
    rows = jnp.arange(TOKENS)
    positions = (block_order[rows // BL] * BL + rows % BL).astype(jnp.int32)
    query = rope(jnp.dot(normed, w_query, preferred_element_type=jnp.float32), positions, HEADS).astype(jnp.bfloat16)
    keys = rope(jnp.dot(normed, w_key, preferred_element_type=jnp.float32), positions, KVH).astype(jnp.bfloat16)
    values = jnp.dot(normed, w_value, preferred_element_type=jnp.float32).astype(jnp.bfloat16)
    allowed = positions[None, :] <= positions[:, None]
    per_kv = HEADS // KVH

    def one_head(head):
        group = head // per_kv
        qh = lax.dynamic_slice_in_dim(query, (head * HD).astype(jnp.int32), HD, 1)
        kh = lax.dynamic_slice_in_dim(keys, (group * HD).astype(jnp.int32), HD, 1)
        vh = lax.dynamic_slice_in_dim(values, (group * HD).astype(jnp.int32), HD, 1)
        score = jnp.einsum('qd,kd->qk', qh.astype(jnp.float32), kh.astype(jnp.float32)) / jnp.sqrt(jnp.float32(HD))
        score = jnp.where(allowed, score, -1e+30)
        probs = jax.nn.softmax(score, axis=1).astype(jnp.bfloat16)
        return jnp.dot(probs, vh, preferred_element_type=jnp.float32).astype(jnp.bfloat16)
    attended = lax.map(one_head, jnp.arange(HEADS).astype(jnp.int32))
    attended = jnp.transpose(attended, (1, 0, 2)).reshape(TOKENS, HEADS * HD)
    span = HEAD_DEV * HD

    def add_group(total, group):
        part = lax.dynamic_slice_in_dim(attended, (group * span).astype(jnp.int32), span, 1)
        rows_w = lax.dynamic_slice_in_dim(w_out, (group * span).astype(jnp.int32), span, 0)
        term = jnp.dot(part, rows_w, preferred_element_type=jnp.float32)
        coded, scale = encode(rotate_rows(term, sgn, mat), BLK)
        back = coded.astype(jnp.float32).reshape(TOKENS, NBD, BLK) * scale.astype(jnp.float32)[:, :, None]
        return (total + back.reshape(TOKENS, D), None)
    summed, _ = lax.scan(add_group, jnp.zeros((TOKENS, D), jnp.float32), jnp.arange(N_TENSOR).astype(jnp.int32))
    newres = resid + unrotate_rows(summed, sgn, mat)
    out_coded, out_scale = encode(rotate_rows(newres, sgn, mat), BLK)
    return (out_coded, out_scale.T)
```

```python
import functools
import math

import jax
import jax.numpy as jnp
from jax import lax
from jax.experimental import pallas as pl
from jax.experimental.pallas import tpu as pltpu
from jax.sharding import PartitionSpec as P

HD = 128
KVH = 8
BLK = 128
NBLOCK = 16


HIGH = lax.Precision.HIGHEST


def hadamard(width):
    idx = jnp.arange(width)
    parity = jnp.zeros((width, width), jnp.int32)
    bit = 1
    while bit < width:
        parity = parity + idx[:, None] // bit % 2 * (idx[None, :] // bit % 2)
        bit = bit * 2
    return jnp.where(parity % 2 == 0, 1.0, -1.0).astype(jnp.float32) / jnp.sqrt(jnp.float32(width))


def rotate_rows(value, sgn, mat):
    rows = value.shape[0]
    blocks = (value * sgn).reshape(rows, -1, mat.shape[0])
    return jnp.einsum("tnb,bc->tnc", blocks, mat, precision=HIGH).reshape(rows, -1)


def unrotate_rows(value, sgn, mat):
    rows = value.shape[0]
    blocks = value.reshape(rows, -1, mat.shape[0])
    return jnp.einsum("tnb,bc->tnc", blocks, mat, precision=HIGH).reshape(rows, -1) * sgn


def rope(value, positions, heads):
    rows = value.shape[0]
    half = HD // 2
    freqs = 500000.0 ** (-(jnp.arange(half).astype(jnp.float32) * 2.0) / HD)
    angle = positions.astype(jnp.float32)[:, None] * freqs[None, :]
    cosine = jnp.cos(angle)[:, None, :]
    sine = jnp.sin(angle)[:, None, :]
    parts = value.reshape(rows, heads, HD)
    first = parts[:, :, :half]
    second = parts[:, :, half:]
    out = jnp.concatenate([first * cosine - second * sine, second * cosine + first * sine], axis=2)
    return out.reshape(rows, heads * HD)


def encode_pairs(joined, positions):
    width = KVH * HD
    keys = rope(joined[:, :width], positions, KVH)
    return jnp.concatenate([keys, joined[:, width:]], axis=1).astype(jnp.bfloat16)


def attend(query_head, key_head, value_head, allowed):
    score = jnp.einsum(
        "qd,kd->qk", query_head, key_head, preferred_element_type=jnp.float32
    ) / jnp.sqrt(jnp.float32(HD))
    score = jnp.where(allowed, score, -1e30)
    probs = jax.nn.softmax(score, axis=1).astype(jnp.bfloat16)
    return jnp.dot(probs, value_head, preferred_element_type=jnp.float32).astype(jnp.bfloat16)


def general(x_coded, x_scales, signs, block_order, norm_gain, w_query, w_key, w_value, w_out):
    count = lax.axis_size("tensor")
    index = lax.axis_index("tensor")
    mat = hadamard(BLK)
    sgn = (2 * signs - 1).astype(jnp.float32)
    coded_all, scales_all = (
        lax.all_gather(x_coded, "tensor", axis=1, tiled=True),
        lax.all_gather(x_scales, "tensor", axis=0, tiled=True),
    )
    tokens = coded_all.shape[0]
    nblocks = scales_all.shape[0]
    deq = (
        coded_all.astype(jnp.float32).reshape(tokens, nblocks, BLK)
        * scales_all.astype(jnp.float32).T[:, :, None]
    )
    resid = unrotate_rows(deq.reshape(tokens, -1), sgn, mat)
    inv = lax.rsqrt(jnp.mean(resid * resid, axis=1, keepdims=True) + 1e-05)
    normed = (resid * norm_gain.astype(jnp.float32) * inv).astype(jnp.bfloat16)
    rows = jnp.arange(tokens)
    blen = tokens // NBLOCK
    positions = block_order[rows // blen] * blen + rows % blen
    heads_here = w_query.shape[1] // HD
    query = rope(
        jnp.dot(normed, w_query, preferred_element_type=jnp.float32), positions, heads_here
    ).astype(jnp.bfloat16)
    width = w_key.shape[0]
    mine = lax.dynamic_slice_in_dim(normed, index * width, width, 1)
    joined_w = jnp.concatenate([w_key, w_value], axis=1)
    kv_part = jnp.dot(mine, joined_w, preferred_element_type=jnp.float32)
    share = lax.psum_scatter(kv_part, "tensor", scatter_dimension=0, tiled=True)
    share_rows = share.shape[0]
    share_pos = lax.dynamic_slice_in_dim(positions, index * share_rows, share_rows, 0)
    keyval = lax.all_gather(encode_pairs(share, share_pos), "tensor", axis=0, tiled=True)
    allowed = positions[None, :] <= positions[:, None]
    per_kv = heads_here * count // KVH
    head = index * heads_here + 0
    group = head // per_kv
    key_head = lax.dynamic_slice_in_dim(keyval, group * HD, HD, 1)
    value_head = lax.dynamic_slice_in_dim(keyval, KVH * HD + group * HD, HD, 1)
    outputs = attend(query, key_head, value_head, allowed)
    rotated_w = rotate_rows(w_out.astype(jnp.float32), sgn, mat)
    rotated = jnp.dot(outputs.astype(jnp.float32), rotated_w, precision=HIGH)
    blocks = rotated.reshape(tokens, nblocks, BLK)
    scale = (jnp.max(jnp.abs(blocks), axis=2) + 1e-06).astype(jnp.bfloat16)
    coded = (blocks / scale.astype(jnp.float32)[:, :, None]).astype(jnp.bfloat16)
    send_vals = coded.reshape(tokens, count, width)
    send_scale = scale.reshape(tokens, count, nblocks // count)
    got_vals, got_scale = (
        lax.all_to_all(send_vals, "tensor", split_axis=1, concat_axis=1, tiled=True),
        lax.all_to_all(send_scale, "tensor", split_axis=1, concat_axis=1, tiled=True),
    )
    back = (
        got_vals.astype(jnp.float32).reshape(tokens, count, width // BLK, BLK)
        * got_scale.astype(jnp.float32)[:, :, :, None]
    )
    summed = jnp.sum(back, axis=1).reshape(tokens, width)
    sgn_mine = lax.dynamic_slice_in_dim(sgn, index * width, width, 0)
    resid_mine = lax.dynamic_slice_in_dim(resid, index * width, width, 1)
    newres = resid_mine + unrotate_rows(summed, sgn_mine, mat)
    final = rotate_rows(newres, sgn_mine, mat).reshape(tokens, width // BLK, BLK)
    out_scale = (jnp.max(jnp.abs(final), axis=2) + 1e-06).astype(jnp.bfloat16)
    out_coded = (final / out_scale.astype(jnp.float32)[:, :, None]).astype(jnp.bfloat16)
    return (out_coded.reshape(tokens, width), out_scale.T)


def spin(rows, cols):
    i = lax.broadcasted_iota(jnp.int32, (rows, cols), 0)
    j = lax.broadcasted_iota(jnp.int32, (rows, cols), 1)
    v = i & j
    v = v ^ (v >> 4)
    v = v ^ (v >> 2)
    v = v ^ (v >> 1)
    return (1 - 2 * (v & 1)).astype(jnp.float32).astype(jnp.bfloat16)


def dot(a, b):
    return jnp.dot(a, b, preferred_element_type=jnp.float32)


def call(kernel, outs, args, specs, out_specs, prefetch, scratch=(), flops=10**8, nbytes=10**6):
    return pl.pallas_call(
        kernel,
        out_shape=outs,
        grid_spec=pltpu.PrefetchScalarGridSpec(
            num_scalar_prefetch=1,
            grid=(1,),
            in_specs=specs,
            out_specs=out_specs,
            scratch_shapes=scratch,
        ),
        compiler_params=pltpu.CompilerParams(vmem_limit_bytes=40 * 2**20),
        cost_estimate=pl.CostEstimate(flops=flops, bytes_accessed=nbytes, transcendentals=0),
    )(prefetch, *args)


def whole(shape):
    return pl.BlockSpec(shape, lambda i, me: (0,) * len(shape))


def rows_of(shape, rel):
    return pl.BlockSpec(shape, lambda i, me: (me[0] ^ rel, 0))


def cols_of(shape, rel):
    return pl.BlockSpec(shape, lambda i, me: (0, me[0] ^ rel))


def lead_of(shape, rel):
    return pl.BlockSpec(shape, lambda i, me: (me[0] ^ rel, 0, 0))


def unrotate_kernel(me, x_ref, s_ref, sg_ref, u_ref):
    had = spin(BLK, BLK)
    scale = s_ref[...].astype(jnp.float32).T
    for b in range(x_ref.shape[1] // BLK):
        at = slice(b * BLK, (b + 1) * BLK)
        part = dot(x_ref[:, at], had) * scale[:, b : b + 1]
        u_ref[:, at] = (part * sg_ref[0:1, at]).astype(jnp.bfloat16)


def keyval_kernel(me, u_ref, wk_ref, wv_ref, send_ref, keep_ref, first, second, sems):
    core = me[0] & 1
    chip = me[0] >> 1

    @pl.when(core == 0)
    def _():
        pltpu.make_async_copy(wv_ref, first, sems.at[0]).start()
        pltpu.make_async_copy(wk_ref, second, sems.at[1]).start()

    @pl.when(core == 1)
    def _():
        pltpu.make_async_copy(wk_ref, first, sems.at[0]).start()
        pltpu.make_async_copy(wv_ref, second, sems.at[1]).start()

    for at, (held, out) in enumerate(((first, send_ref), (second, keep_ref))):
        pltpu.make_async_copy(wk_ref, held, sems.at[at]).wait()
        part = dot(u_ref[...], held[...]).astype(jnp.bfloat16)
        for p in range(KVH):
            rel = chip ^ p
            out[rel & 1, rel >> 1] = part[:, p * HD : (p + 1) * HD]


def query_kernel(n, begins, me, *refs):
    us, refs = refs[:n], refs[n:]
    ws, refs = refs[:n], refs[n:]
    xs, refs = refs[:n], refs[n:]
    gs, refs = refs[:n], refs[n:]
    if begins:
        own, other, square = 0.0, 0.0, 0.0
    else:
        own, other, square = refs[0][...], refs[1][:, :HD], refs[1][:, HD:]
        refs = refs[2:]
    own_ref, pay_ref = refs
    for u_ref, w_ref, x_ref, g_ref in zip(us, ws, xs, gs):
        u = u_ref[...]
        own = own + dot(u, w_ref[...])
        other = other + dot(u, x_ref[...])
        for b in range(u.shape[1] // BLK):
            at = slice(b * BLK, (b + 1) * BLK)
            r = u[:, at].astype(jnp.float32) * g_ref[0, :, at]
            square = square + r * r
    own_ref[...] = own
    pay_ref[:, :HD] = other
    pay_ref[:, HD:] = square


def turn(value, cosine, sine):
    half = HD // 2
    swapped = jnp.concatenate([value[:, half:], value[:, :half]], axis=1)
    return (value * cosine + swapped * sine).astype(jnp.bfloat16)


def attend_kernel(width, me, own_ref, pay_ref, got_ref, kv_ref, kvx_ref, cos_ref, sin_ref, row_ref, col_ref, out_ref):
    core = me[0] & 1
    square = jnp.sum(pay_ref[:, HD:] + got_ref[:, HD:], axis=1, keepdims=True)
    inv = lax.rsqrt(square / width + 1e-05)
    cosine, sine = cos_ref[...], sin_ref[...]
    query = turn((own_ref[...] + got_ref[:, :HD]) * inv, cosine, sine)
    mine, theirs = kv_ref[...].astype(jnp.float32), kvx_ref[...].astype(jnp.float32)
    key = turn(jnp.where(core == 0, mine, theirs) * inv, cosine, sine)
    value = (jnp.where(core == 0, theirs, mine) * inv).astype(jnp.bfloat16)
    score = lax.dot_general(query, key, (((1,), (1,)), ((), ())), preferred_element_type=jnp.float32)
    score = jnp.where(row_ref[...] <= col_ref[...], score / math.sqrt(HD), -1e30)
    weight = jnp.exp(score - jnp.max(score, axis=1, keepdims=True))
    probs = (weight / jnp.sum(weight, axis=1, keepdims=True)).astype(jnp.bfloat16)
    out_ref[...] = dot(probs, value).astype(jnp.bfloat16)


def term_kernel(n, adds, me, a_ref, b_ref, *refs):
    for k in range(n):
        term = dot(a_ref[...], refs[k][...]) + dot(b_ref[...], refs[n + k][...])
        if adds:
            term = term + refs[2 * n + k][...].astype(jnp.float32)
        refs[-n + k][...] = term.astype(jnp.bfloat16)


def final_kernel(n, me, a_ref, b_ref, w_ref, wx_ref, x_ref, s_ref, sg_ref, *refs):
    had = spin(BLK, BLK)
    scale = s_ref[...].astype(jnp.float32).T
    total = dot(a_ref[...], w_ref[...]) + dot(b_ref[...], wx_ref[...])
    for ref in refs[:n]:
        total = total + ref[...].astype(jnp.float32)
    coded_ref, scales_ref = refs[n:]
    total = total * (sg_ref[1:2, :] / math.sqrt(BLK))
    tops = []
    for b in range(x_ref.shape[1] // BLK):
        at = slice(b * BLK, (b + 1) * BLK)
        part = total[:, at]
        high = part.astype(jnp.bfloat16)
        part = part - high.astype(jnp.float32)
        mid = part.astype(jnp.bfloat16)
        low = (part - mid.astype(jnp.float32)).astype(jnp.bfloat16)
        new = dot(high, had) + (dot(mid, had) + dot(low, had))
        new = new + x_ref[:, at].astype(jnp.float32) * scale[:, b : b + 1]
        top = (jnp.max(jnp.abs(new), axis=1, keepdims=True) + 1e-06).astype(jnp.bfloat16).astype(jnp.float32)
        coded_ref[:, at] = (new / top).astype(jnp.bfloat16)
        tops.append(top)
    scales_ref[...] = jnp.concatenate(tops, axis=1).T.astype(jnp.bfloat16)


def swap(value, rel):
    count = lax.axis_size("tensor")
    return lax.ppermute(value, "tensor", [(i, i ^ rel) for i in range(count)])


CORE, ACROSS = 1, 2


def paired(x_coded, x_scales, signs, block_order, norm_gain, w_query, w_key, w_value, w_out):
    count = lax.axis_size("tensor")
    index = lax.axis_index("tensor")
    me = jnp.reshape(index, (1,)).astype(jnp.int32)
    tokens, width = x_coded.shape
    bf16, f32 = jnp.bfloat16, jnp.float32
    sgn = (2 * lax.dynamic_slice_in_dim(signs, index * width, width, 0) - 1).astype(f32)
    gain_mine = lax.dynamic_slice_in_dim(norm_gain, index * width, width, 0).astype(f32)
    sg = jnp.stack([sgn * gain_mine * (1.0 / math.sqrt(BLK)), sgn])
    block = (tokens, width)
    u = call(
        unrotate_kernel,
        jax.ShapeDtypeStruct(block, bf16),
        (x_coded, x_scales, sg),
        [whole(block), whole(x_scales.shape), whole(sg.shape)],
        whole(block),
        me,
    )
    wq_other = swap(w_query, CORE)
    wo_other = swap(w_out, CORE)

    chunk = {0: u}
    for rel in (2, 4, 8, 12):
        chunk[rel] = swap(u, rel)
    for rel in (6, 10, 14):
        chunk[rel] = swap(chunk[rel - 2], ACROSS)

    pieces = (2, KVH // 2, tokens, HD)
    send, keep = call(
        keyval_kernel,
        (jax.ShapeDtypeStruct(pieces, bf16),) * 2,
        (u, w_key, w_value),
        [whole(block), pl.BlockSpec(memory_space=pl.ANY), pl.BlockSpec(memory_space=pl.ANY)],
        (whole(pieces), whole(pieces)),
        me,
        scratch=[pltpu.VMEM(w_key.shape, bf16), pltpu.VMEM(w_key.shape, bf16), pltpu.SemaphoreType.DMA((2,))],
    )

    def plus(a, b):
        return (a.astype(f32) + b.astype(f32)).astype(bf16)

    kv = plus(keep, swap(send, CORE))
    kv = plus(kv[0], swap(kv[1], ACROSS))
    kv = plus(kv[0::2], swap(kv[1::2], 4))
    kv = plus(kv[0], swap(kv[1], 8))
    kv_other = swap(kv, CORE)

    ginv = (1.0 / norm_gain.astype(f32)).reshape(count, 1, width)

    def query(rels, before):
        n = len(rels)
        shapes = ((tokens, HD), (tokens, 2 * HD))
        return call(
            functools.partial(query_kernel, n, before is None),
            tuple(jax.ShapeDtypeStruct(s, f32) for s in shapes),
            tuple(chunk[r] for r in rels) + (w_query,) * n + (wq_other,) * n + (ginv,) * n + (before or ()),
            [whole(block)] * n
            + [rows_of((width, HD), r) for r in rels] * 2
            + [lead_of((1, 1, width), r) for r in rels]
            + ([whole(s) for s in shapes] if before else []),
            tuple(whole(s) for s in shapes),
            me,
        )

    before = query((0, 2, 4, 6), None)
    own, pay = query((8, 10, 12, 14), before)
    got = swap(pay, CORE)

    blen = tokens // NBLOCK
    positions = (block_order[:, None] * blen + jnp.arange(blen)[None, :]).reshape(-1)
    half = HD // 2
    freqs = 500000.0 ** (-(jnp.arange(half).astype(f32) * 2.0) / HD)
    angle = positions.astype(f32)[:, None] * freqs[None, :]
    cosine, sine = jnp.cos(angle), jnp.sin(angle)
    cosine = jnp.concatenate([cosine, cosine], axis=1)
    sine = jnp.concatenate([-sine, sine], axis=1)
    args = (own, pay, got, kv, kv_other, cosine, sine, positions[None, :], positions[:, None])
    att = call(
        functools.partial(attend_kernel, count * width),
        jax.ShapeDtypeStruct((tokens, HD), bf16),
        args,
        [whole(a.shape) for a in args],
        whole((tokens, HD)),
        me,
    )
    att_other = swap(att, CORE)

    def terms(rels, adds):
        n = len(rels)
        return call(
            functools.partial(term_kernel, n, bool(adds)),
            (jax.ShapeDtypeStruct(block, bf16),) * n,
            (att, att_other) + (w_out,) * n + (wo_other,) * n + tuple(adds),
            [whole(att.shape)] * 2 + [cols_of((HD, width), r) for r in rels] * 2 + [whole(block)] * len(adds),
            (whole(block),) * n,
            me,
        )

    order = (12, 8, 4, 0)
    crossing = terms([r ^ ACROSS for r in order], ())
    landed = []
    for rel, part in zip(order, crossing):
        got = swap(part, ACROSS)
        if rel:
            (part,) = terms([rel], [got])
            got = swap(part, rel)
        landed.append(got)
    n = len(landed)
    return call(
        functools.partial(final_kernel, n),
        (jax.ShapeDtypeStruct(block, bf16), jax.ShapeDtypeStruct(x_scales.shape, bf16)),
        (att, att_other, w_out, wo_other, x_coded, x_scales, sg) + tuple(landed),
        [whole(att.shape)] * 2
        + [cols_of((HD, width), 0)] * 2
        + [whole(block), whole(x_scales.shape), whole(sg.shape)]
        + [whole(block)] * n,
        (whole(block), whole(x_scales.shape)),
        me,
    )


def per_device(*args):
    if lax.axis_size("tensor") == 16:
        return paired(*args)
    return general(*args)


def solution(mesh):
    in_specs = (
        P("group", "tensor"),
        P("tensor", "group"),
        P(),
        P("group"),
        P(),
        P(None, "tensor"),
        P("tensor", None),
        P("tensor", None),
        P("tensor", None),
    )
    out_specs = (P("group", "tensor"), P("tensor", "group"))
    return jax.shard_map(
        per_device, mesh=mesh, in_specs=in_specs, out_specs=out_specs, check_vma=False
    )
```

```python
import functools
import math

import jax
import jax.numpy as jnp
from jax import lax
from jax.experimental import pallas as pl
from jax.experimental.pallas import tpu as pltpu
from jax.sharding import PartitionSpec as P

HD = 128
KVH = 8
BLK = 128
NBLOCK = 16


HIGH = lax.Precision.HIGHEST


def hadamard(width):
    idx = jnp.arange(width)
    parity = jnp.zeros((width, width), jnp.int32)
    bit = 1
    while bit < width:
        parity = parity + idx[:, None] // bit % 2 * (idx[None, :] // bit % 2)
        bit = bit * 2
    return jnp.where(parity % 2 == 0, 1.0, -1.0).astype(jnp.float32) / jnp.sqrt(jnp.float32(width))


def rotate_rows(value, sgn, mat):
    rows = value.shape[0]
    blocks = (value * sgn).reshape(rows, -1, mat.shape[0])
    return jnp.einsum("tnb,bc->tnc", blocks, mat, precision=HIGH).reshape(rows, -1)


def unrotate_rows(value, sgn, mat):
    rows = value.shape[0]
    blocks = value.reshape(rows, -1, mat.shape[0])
    return jnp.einsum("tnb,bc->tnc", blocks, mat, precision=HIGH).reshape(rows, -1) * sgn


def rope(value, positions, heads):
    rows = value.shape[0]
    half = HD // 2
    freqs = 500000.0 ** (-(jnp.arange(half).astype(jnp.float32) * 2.0) / HD)
    angle = positions.astype(jnp.float32)[:, None] * freqs[None, :]
    cosine = jnp.cos(angle)[:, None, :]
    sine = jnp.sin(angle)[:, None, :]
    parts = value.reshape(rows, heads, HD)
    first = parts[:, :, :half]
    second = parts[:, :, half:]
    out = jnp.concatenate([first * cosine - second * sine, second * cosine + first * sine], axis=2)
    return out.reshape(rows, heads * HD)


def encode_pairs(joined, positions):
    width = KVH * HD
    keys = rope(joined[:, :width], positions, KVH)
    return jnp.concatenate([keys, joined[:, width:]], axis=1).astype(jnp.bfloat16)


def attend(query_head, key_head, value_head, allowed):
    score = jnp.einsum(
        "qd,kd->qk", query_head, key_head, preferred_element_type=jnp.float32
    ) / jnp.sqrt(jnp.float32(HD))
    score = jnp.where(allowed, score, -1e30)
    probs = jax.nn.softmax(score, axis=1).astype(jnp.bfloat16)
    return jnp.dot(probs, value_head, preferred_element_type=jnp.float32).astype(jnp.bfloat16)


def general(x_coded, x_scales, signs, block_order, norm_gain, w_query, w_key, w_value, w_out):
    count = lax.axis_size("tensor")
    index = lax.axis_index("tensor")
    mat = hadamard(BLK)
    sgn = (2 * signs - 1).astype(jnp.float32)
    coded_all, scales_all = (
        lax.all_gather(x_coded, "tensor", axis=1, tiled=True),
        lax.all_gather(x_scales, "tensor", axis=0, tiled=True),
    )
    tokens = coded_all.shape[0]
    nblocks = scales_all.shape[0]
    deq = (
        coded_all.astype(jnp.float32).reshape(tokens, nblocks, BLK)
        * scales_all.astype(jnp.float32).T[:, :, None]
    )
    resid = unrotate_rows(deq.reshape(tokens, -1), sgn, mat)
    inv = lax.rsqrt(jnp.mean(resid * resid, axis=1, keepdims=True) + 1e-05)
    normed = (resid * norm_gain.astype(jnp.float32) * inv).astype(jnp.bfloat16)
    rows = jnp.arange(tokens)
    blen = tokens // NBLOCK
    positions = block_order[rows // blen] * blen + rows % blen
    heads_here = w_query.shape[1] // HD
    query = rope(
        jnp.dot(normed, w_query, preferred_element_type=jnp.float32), positions, heads_here
    ).astype(jnp.bfloat16)
    width = w_key.shape[0]
    mine = lax.dynamic_slice_in_dim(normed, index * width, width, 1)
    joined_w = jnp.concatenate([w_key, w_value], axis=1)
    kv_part = jnp.dot(mine, joined_w, preferred_element_type=jnp.float32)
    share = lax.psum_scatter(kv_part, "tensor", scatter_dimension=0, tiled=True)
    share_rows = share.shape[0]
    share_pos = lax.dynamic_slice_in_dim(positions, index * share_rows, share_rows, 0)
    keyval = lax.all_gather(encode_pairs(share, share_pos), "tensor", axis=0, tiled=True)
    allowed = positions[None, :] <= positions[:, None]
    per_kv = heads_here * count // KVH
    head = index * heads_here + 0
    group = head // per_kv
    key_head = lax.dynamic_slice_in_dim(keyval, group * HD, HD, 1)
    value_head = lax.dynamic_slice_in_dim(keyval, KVH * HD + group * HD, HD, 1)
    outputs = attend(query, key_head, value_head, allowed)
    rotated_w = rotate_rows(w_out.astype(jnp.float32), sgn, mat)
    rotated = jnp.dot(outputs.astype(jnp.float32), rotated_w, precision=HIGH)
    blocks = rotated.reshape(tokens, nblocks, BLK)
    scale = (jnp.max(jnp.abs(blocks), axis=2) + 1e-06).astype(jnp.bfloat16)
    coded = (blocks / scale.astype(jnp.float32)[:, :, None]).astype(jnp.bfloat16)
    send_vals = coded.reshape(tokens, count, width)
    send_scale = scale.reshape(tokens, count, nblocks // count)
    got_vals, got_scale = (
        lax.all_to_all(send_vals, "tensor", split_axis=1, concat_axis=1, tiled=True),
        lax.all_to_all(send_scale, "tensor", split_axis=1, concat_axis=1, tiled=True),
    )
    back = (
        got_vals.astype(jnp.float32).reshape(tokens, count, width // BLK, BLK)
        * got_scale.astype(jnp.float32)[:, :, :, None]
    )
    summed = jnp.sum(back, axis=1).reshape(tokens, width)
    sgn_mine = lax.dynamic_slice_in_dim(sgn, index * width, width, 0)
    resid_mine = lax.dynamic_slice_in_dim(resid, index * width, width, 1)
    newres = resid_mine + unrotate_rows(summed, sgn_mine, mat)
    final = rotate_rows(newres, sgn_mine, mat).reshape(tokens, width // BLK, BLK)
    out_scale = (jnp.max(jnp.abs(final), axis=2) + 1e-06).astype(jnp.bfloat16)
    out_coded = (final / out_scale.astype(jnp.float32)[:, :, None]).astype(jnp.bfloat16)
    return (out_coded.reshape(tokens, width), out_scale.T)


def spin(rows, cols):
    i = lax.broadcasted_iota(jnp.int32, (rows, cols), 0)
    j = lax.broadcasted_iota(jnp.int32, (rows, cols), 1)
    v = i & j
    v = v ^ (v >> 4)
    v = v ^ (v >> 2)
    v = v ^ (v >> 1)
    return (1 - 2 * (v & 1)).astype(jnp.float32).astype(jnp.bfloat16)


def dot(a, b):
    return jnp.dot(a, b, preferred_element_type=jnp.float32)


VMEM = pl.BlockSpec(memory_space=pltpu.VMEM)
SMEM = pl.BlockSpec(memory_space=pltpu.SMEM)
HBM = pl.BlockSpec(memory_space=pltpu.HBM)
ANY = pl.BlockSpec(memory_space=pl.ANY)


def call(kernel, outs, args, specs, scratch=(), micros=1):
    many = isinstance(outs, tuple)
    args = [pltpu.with_memory_space_constraint(a, pltpu.HBM) if spec is HBM else a for a, spec in zip(args, specs)]
    return pl.pallas_call(
        kernel,
        out_shape=outs,
        in_specs=specs,
        out_specs=(VMEM,) * len(outs) if many else VMEM,
        scratch_shapes=scratch,
        compiler_params=pltpu.CompilerParams(vmem_limit_bytes=32 * 2**20),
        cost_estimate=pl.CostEstimate(flops=micros * 10**9, bytes_accessed=10**6, transcendentals=0),
    )(*args)


def fetch(pairs, sems):
    copies = [pltpu.make_async_copy(src, dst, sems.at[k]) for k, (src, dst) in enumerate(pairs)]
    for copy in copies:
        copy.start()
    return copies


def unrotate_kernel(
    me, x_hbm, s_hbm, sign_hbm, gain_hbm, u_ref, x, s, sign, gain, held, sems
):
    per = sign.shape[0]
    at = pl.multiple_of(me[0] * per, per)
    copies = fetch(
        ((gain_hbm, gain), (sign_hbm.at[pl.ds(at, per), :], sign), (s_hbm, s), (x_hbm, x)),
        sems,
    )

    had = spin(BLK, BLK)
    copies[0].wait()
    held[...] = gain[...].astype(jnp.float32)
    copies[1].wait()
    sg = held[pl.ds(at, per), :] * ((2 * sign[...] - 1).astype(jnp.float32) / math.sqrt(BLK))
    copies[2].wait()
    scale = s[...].astype(jnp.float32).T
    copies[3].wait()
    for b in range(per):
        cols = slice(b * BLK, (b + 1) * BLK)
        part = dot(x[:, cols], had) * scale[:, b : b + 1]
        u_ref[:, cols] = (part * sg[b : b + 1, :]).astype(jnp.bfloat16)


def token_kernel(*refs):
    refs[-1][...] = jnp.zeros_like(refs[-1])


def keyval_kernel(me, u_ref, wk_hbm, wv_hbm, kv_ref, first, second, sems):
    copies = fetch(((wk_hbm, first), (wv_hbm, second)), sems)
    core, chip = me[0] & 1, me[0] >> 1
    for kind, weights in enumerate((first, second)):
        copies[kind].wait()
        part = dot(u_ref[...], weights[...]).astype(jnp.bfloat16)
        for p in range(KVH):
            kv_ref[(chip ^ p) & 1, 1 - (core ^ kind), p >> 1] = part[:, p * HD : (p + 1) * HD]


def joint(me, w_hbm, x_hbm, rel, into):
    width = into.shape[0]
    at = pl.ds(pl.multiple_of((me[0] ^ rel) * width, width), width)
    return [(w_hbm.at[at, :], into.at[:, pl.ds(0, HD)]), (x_hbm.at[at, :], into.at[:, pl.ds(HD, HD)])]


def products(me, rel, u, weights, held):
    per = u.shape[1] // BLK
    inverse = held[pl.ds(pl.multiple_of((me[0] ^ rel) * per, per), per), :]
    square = 0.0
    for b in range(per):
        r = u[:, b * BLK : (b + 1) * BLK].astype(jnp.float32) * inverse[b : b + 1, :]
        square = square + r * r
    return dot(u, weights), square


def query_kernel(rels, me, token, gain_ref, w_hbm, x_hbm, *refs):
    n = len(rels)
    us, (pay_ref, ws, held, sems) = refs[:n], refs[n:]
    pairs = []
    for k, rel in enumerate(rels):
        pairs += joint(me, w_hbm, x_hbm, rel, ws.at[k])
    copies = fetch(pairs, sems)
    held[...] = 1.0 / gain_ref[...].astype(jnp.float32)
    pay, square = 0.0, 0.0
    for k, rel in enumerate(rels):
        copies[2 * k].wait()
        copies[2 * k + 1].wait()
        part, squares = products(me, rel, us[k][...], ws[k], held)
        pay, square = pay + part, square + squares
    pay_ref[:, : 2 * HD] = pay
    pay_ref[:, 2 * HD :] = square


def more_kernel(rels, ahead, me, done, gain_ref, w_hbm, x_hbm, before_ref, *refs):
    n = len(rels)
    us, (pay_ref, ahead_ref, ws, held, sems) = refs[:n], refs[n:]
    pairs = []
    for k, rel in enumerate(rels):
        pairs += joint(me, w_hbm, x_hbm, rel, ws.at[k])
    for k, rel in enumerate(ahead):
        pairs += joint(me, w_hbm, x_hbm, rel, ahead_ref.at[k])
    copies = fetch(pairs, sems)
    held[...] = 1.0 / gain_ref[...].astype(jnp.float32)
    pay, square = before_ref[:, : 2 * HD], before_ref[:, 2 * HD :]
    for k, rel in enumerate(rels):
        copies[2 * k].wait()
        copies[2 * k + 1].wait()
        part, squares = products(me, rel, us[k][...], ws[k], held)
        pay, square = pay + part, square + squares
    for copy in copies[2 * n :]:
        copy.wait()
    pay_ref[:, : 2 * HD] = pay
    pay_ref[:, 2 * HD :] = square


def last_kernel(rels, me, done, gain_ref, w_ref, before_ref, *refs):
    us, (pay_ref, held) = refs[:-2], refs[-2:]
    held[...] = 1.0 / gain_ref[...].astype(jnp.float32)
    pay, square = before_ref[:, : 2 * HD], before_ref[:, 2 * HD :]
    for k, rel in enumerate(rels):
        part, squares = products(me, rel, us[k][...], w_ref[k], held)
        pay, square = pay + part, square + squares
    pay_ref[:, : 2 * HD] = pay
    pay_ref[:, 2 * HD :] = square


def turn(value, cosine, sine):
    half = HD // 2
    swapped = jnp.concatenate([value[:, half:], value[:, :half]], axis=1)
    return (value * cosine + swapped * sine).astype(jnp.bfloat16)


def columns(me, rel, width):
    return pl.ds(pl.multiple_of((me[0] ^ rel) * width, width), width)


def attend_kernel(total, rels, me, pay_ref, got_ref, kv_ref, kvx_ref, cos_ref, sin_ref, row_ref, col_ref, w_hbm, x_hbm, *refs):
    att_ref, outs, (ws, xs, sems) = refs[0], refs[1:-3], refs[-3:]
    width = ws.shape[2]
    copies = fetch(
        [(src.at[:, columns(me, rel, width)], dst.at[k]) for k, rel in enumerate(rels) for src, dst in ((w_hbm, ws), (x_hbm, xs))],
        sems,
    )
    square = jnp.sum(pay_ref[:, 2 * HD :] + got_ref[:, 2 * HD :], axis=1, keepdims=True)
    inv = lax.rsqrt(square / total + 1e-05)
    cosine, sine = cos_ref[...], sin_ref[...]
    core = me[0] & 1
    mine, theirs = kv_ref[...].astype(jnp.float32), kvx_ref[...].astype(jnp.float32)
    key = turn(jnp.where(core == 0, mine, theirs) * inv, cosine, sine)
    value = (jnp.where(core == 0, theirs, mine) * inv).astype(jnp.bfloat16)
    allowed = row_ref[...] <= col_ref[...]
    heads = []
    for at in range(2):
        query = pay_ref[:, at * HD : (at + 1) * HD] + got_ref[:, (1 - at) * HD : (2 - at) * HD]
        query = turn(query * inv, cosine, sine)
        score = lax.dot_general(query, key, (((1,), (1,)), ((), ())), preferred_element_type=jnp.float32)
        score = jnp.where(allowed, score / math.sqrt(HD), -1e30)
        weight = jnp.exp(score - jnp.max(score, axis=1, keepdims=True))
        probs = (weight / jnp.sum(weight, axis=1, keepdims=True)).astype(jnp.bfloat16)
        head = dot(probs, value).astype(jnp.bfloat16)
        att_ref[:, at * HD : (at + 1) * HD] = head
        heads.append(head)
    for k, out in enumerate(outs):
        copies[2 * k].wait()
        copies[2 * k + 1].wait()
        out[...] = (dot(heads[0], ws[k]) + dot(heads[1], xs[k])).astype(out.dtype)


def term_kernel(rels, added, me, done, att_ref, w_hbm, x_hbm, *refs):
    adds, outs, (ws, xs, sems) = refs[:added], refs[added:-3], refs[-3:]
    width = ws.shape[2]
    copies = fetch(
        [(src.at[:, columns(me, rel, width)], dst.at[k]) for k, rel in enumerate(rels) for src, dst in ((w_hbm, ws), (x_hbm, xs))],
        sems,
    )
    for k, out in enumerate(outs):
        copies[2 * k].wait()
        copies[2 * k + 1].wait()
        term = dot(att_ref[:, :HD], ws[k]) + dot(att_ref[:, HD:], xs[k])
        if k < added:
            term = term + adds[k][...].astype(jnp.float32)
        out[...] = term.astype(out.dtype)


def final_kernel(n, me, done, x_ref, s_ref, sign_ref, *refs):
    had = spin(BLK, BLK)
    scale = s_ref[...].astype(jnp.float32).T
    per = s_ref.shape[0]
    sign = (2 * sign_ref[pl.ds(pl.multiple_of(me[0] * per, per), per), :] - 1).astype(jnp.float32) / math.sqrt(BLK)
    parts, (coded_ref, scales_ref) = refs[:n], refs[n:]
    tops = []
    for b in range(per):
        at = slice(b * BLK, (b + 1) * BLK)
        part = parts[0][:, at].astype(jnp.float32)
        for ref in parts[1:]:
            part = part + ref[:, at].astype(jnp.float32)
        part = part * sign[b : b + 1, :]
        high = part.astype(jnp.bfloat16)
        part = part - high.astype(jnp.float32)
        mid = part.astype(jnp.bfloat16)
        low = (part - mid.astype(jnp.float32)).astype(jnp.bfloat16)
        new = dot(high, had) + (dot(mid, had) + dot(low, had))
        new = new + x_ref[:, at].astype(jnp.float32) * scale[:, b : b + 1]
        top = (jnp.max(jnp.abs(new), axis=1, keepdims=True) + 1e-06).astype(jnp.bfloat16).astype(jnp.float32)
        coded_ref[:, at] = (new / top).astype(jnp.bfloat16)
        tops.append(top)
    scales_ref[...] = jnp.concatenate(tops, axis=1).T.astype(jnp.bfloat16)


def swap(value, rel):
    count = lax.axis_size("tensor")
    return lax.ppermute(value, "tensor", [(i, i ^ rel) for i in range(count)])


CORE, ACROSS, NEAR, FAR = 1, 2, 4, 8


def paired(x_coded, x_scales, signs, block_order, norm_gain, w_query, w_key, w_value, w_out):
    count = lax.axis_size("tensor")
    index = lax.axis_index("tensor")
    me = jnp.reshape(index, (1,)).astype(jnp.int32)
    tokens, width = x_coded.shape
    bf16, f32 = jnp.bfloat16, jnp.float32
    block = jax.ShapeDtypeStruct((tokens, width), bf16)
    wide = jax.ShapeDtypeStruct((tokens, width), f32)
    dma = pltpu.SemaphoreType.DMA
    together = lax.optimization_barrier
    sign2 = signs.reshape(-1, BLK)
    gain2 = norm_gain.reshape(-1, BLK)
    u = call(
        unrotate_kernel,
        block,
        (me, x_coded, x_scales, sign2, gain2),
        [SMEM] + [HBM] * 4,
        [
            pltpu.VMEM(x_coded.shape, bf16),
            pltpu.VMEM(x_scales.shape, bf16),
            pltpu.VMEM((width // BLK, BLK), jnp.int32),
            pltpu.VMEM(gain2.shape, bf16),
            pltpu.VMEM(gain2.shape, f32),
            dma((4,)),
        ],
    )
    wq_other = swap(w_query, CORE)
    chunk = {0: u, FAR: swap(u, FAR)}
    kv = call(
        keyval_kernel,
        jax.ShapeDtypeStruct((2, 2, KVH // 2, tokens, HD), bf16),
        (me, u, w_key, w_value),
        [SMEM, VMEM, HBM, HBM],
        [pltpu.VMEM(w_key.shape, bf16), pltpu.VMEM(w_key.shape, bf16), dma((2,))],
        micros=20,
    )

    def plus(*parts):
        return sum(p.astype(f32) for p in parts).astype(bf16)

    def after(*arrays):
        return call(token_kernel, jax.ShapeDtypeStruct((8, BLK), f32), arrays, [ANY] * len(arrays), micros=3)

    chunk[ACROSS] = swap(u, ACROSS)
    chunk[NEAR] = swap(u, NEAR)
    kvx = swap(kv[1], ACROSS)
    done = after(chunk[8], chunk[2], chunk[4])
    done, chunk[8], chunk[2], chunk[4], kvx, wq_other = together((done, chunk[8], chunk[2], chunk[4], kvx, wq_other))
    kv = plus(kv[0], kvx)
    chunk[12] = swap(chunk[8], NEAR)
    chunk[10] = swap(chunk[8], ACROSS)

    partial = jax.ShapeDtypeStruct((tokens, 3 * HD), f32)

    early, more, late = (0, 2, 4), (8, 10, 12), (6, 14)
    pay = call(
        functools.partial(query_kernel, early),
        partial,
        (me, done, gain2, w_query, wq_other) + tuple(chunk[r] for r in early),
        [SMEM, ANY, VMEM, HBM, HBM] + [VMEM] * len(early),
        [
            pltpu.VMEM((len(early), width, 2 * HD), bf16),
            pltpu.VMEM(gain2.shape, f32),
            dma((2 * len(early),)),
        ],
        micros=3,
    )
    kv = plus(kv[1], swap(kv[0], CORE))
    kv, w_out_now = together((kv, w_out))
    wo_other = swap(w_out_now, CORE)
    kv, pay = together((kv, pay))
    alike = [[4 * z + low for z in range(count // 4)] for low in range(4)]
    kv = lax.all_to_all(kv, "tensor", 0, 0, axis_index_groups=alike, tiled=True)
    done = after(chunk[12], chunk[10])
    done, chunk[2], chunk[12], chunk[10], pay = together((done, chunk[2], chunk[12], chunk[10], pay))
    chunk[14] = swap(chunk[12], ACROSS)
    chunk[6] = swap(chunk[2], NEAR)
    pay, ahead = call(
        functools.partial(more_kernel, more, late),
        (partial, jax.ShapeDtypeStruct((len(late), width, 2 * HD), bf16)),
        (me, done, gain2, w_query, wq_other, pay) + tuple(chunk[r] for r in more),
        [SMEM, ANY, VMEM, HBM, HBM, VMEM] + [VMEM] * len(more),
        [
            pltpu.VMEM((len(more), width, 2 * HD), bf16),
            pltpu.VMEM(gain2.shape, f32),
            dma((2 * len(more + late),)),
        ],
        micros=3,
    )
    kv = jnp.sum(kv.astype(f32), axis=0).astype(bf16)
    kv_other = swap(kv, CORE)
    pay = call(
        functools.partial(last_kernel, late),
        partial,
        (me, after(chunk[14], chunk[6]), gain2, ahead, pay) + tuple(chunk[r] for r in late),
        [SMEM, ANY] + [VMEM] * (3 + len(late)),
        [pltpu.VMEM(gain2.shape, f32)],
    )
    got = swap(pay, CORE)

    blen = tokens // NBLOCK
    positions = (block_order[:, None] * blen + jnp.arange(blen)[None, :]).reshape(-1)
    half = HD // 2
    freqs = 500000.0 ** (-(jnp.arange(half).astype(f32) * 2.0) / HD)
    angle = positions.astype(f32)[:, None] * freqs[None, :]
    cosine, sine = jnp.cos(angle), jnp.sin(angle)
    cosine = jnp.concatenate([cosine, cosine], axis=1)
    sine = jnp.concatenate([-sine, sine], axis=1)

    def buffers(n):
        return [pltpu.VMEM((n, HD, width), bf16), pltpu.VMEM((n, HD, width), bf16), dma((2 * n,))]

    args = (me, pay, got, kv, kv_other, cosine, sine, positions[None, :], positions[:, None], w_out, wo_other)
    att, t14, t6 = call(
        functools.partial(attend_kernel, count * width, (14, 6)),
        (jax.ShapeDtypeStruct((tokens, 2 * HD), bf16), block, block),
        args,
        [SMEM] + [VMEM] * 8 + [HBM] * 2,
        buffers(2),
    )

    a14 = swap(t14, ACROSS)
    n6 = swap(t6, NEAR)

    def terms(rels, kinds, done, adds=()):
        return call(
            functools.partial(term_kernel, rels, len(adds)),
            kinds,
            (me, done, att, w_out, wo_other) + adds,
            [SMEM, ANY, VMEM, HBM, HBM] + [VMEM] * len(adds),
            buffers(len(rels)),
            micros=20,
        )

    t10, t4, t12, t8, t0 = terms((10, 4, 12, 8, 0), (block, block, wide, wide, wide), me)
    done, a14, n6, t10 = together((after(a14), a14, n6, t10))
    n12 = swap(plus(t12, a14), NEAR)
    a10 = swap(t10, ACROSS)
    n12, a10, n6, t4 = together((n12, a10, n6, t4))
    n8 = swap(plus(t8, a10, n12), FAR)
    n4 = swap(t4, NEAR)
    (t2,) = terms((2,), (block,), done, (n6,))
    a2 = swap(t2, ACROSS)
    parts = (t0, a2, n4, n8)
    return call(
        functools.partial(final_kernel, len(parts)),
        (block, jax.ShapeDtypeStruct(x_scales.shape, bf16)),
        (me, after(n8), x_coded, x_scales, sign2) + parts,
        [SMEM, ANY] + [VMEM] * (3 + len(parts)),
    )


def per_device(*args):
    if lax.axis_size("tensor") == 16:
        return paired(*args)
    return general(*args)


def solution(mesh):
    in_specs = (
        P("group", "tensor"),
        P("tensor", "group"),
        P(),
        P("group"),
        P(),
        P(None, "tensor"),
        P("tensor", None),
        P("tensor", None),
        P("tensor", None),
    )
    out_specs = (P("group", "tensor"), P("tensor", "group"))
    return jax.shard_map(
        per_device, mesh=mesh, in_specs=in_specs, out_specs=out_specs, check_vma=False
    )
```

```python
import functools
import math

import jax
import jax.numpy as jnp
from jax import lax
from jax.experimental import pallas as pl
from jax.experimental.pallas import tpu as pltpu
from jax.sharding import PartitionSpec as P

HD = 128
KVH = 8
BLK = 128
NBLOCK = 16


HIGH = lax.Precision.HIGHEST


def hadamard(width):
    idx = jnp.arange(width)
    parity = jnp.zeros((width, width), jnp.int32)
    bit = 1
    while bit < width:
        parity = parity + idx[:, None] // bit % 2 * (idx[None, :] // bit % 2)
        bit = bit * 2
    return jnp.where(parity % 2 == 0, 1.0, -1.0).astype(jnp.float32) / jnp.sqrt(jnp.float32(width))


def rotate_rows(value, sgn, mat):
    rows = value.shape[0]
    blocks = (value * sgn).reshape(rows, -1, mat.shape[0])
    return jnp.einsum("tnb,bc->tnc", blocks, mat, precision=HIGH).reshape(rows, -1)


def unrotate_rows(value, sgn, mat):
    rows = value.shape[0]
    blocks = value.reshape(rows, -1, mat.shape[0])
    return jnp.einsum("tnb,bc->tnc", blocks, mat, precision=HIGH).reshape(rows, -1) * sgn


def rope(value, positions, heads):
    rows = value.shape[0]
    half = HD // 2
    freqs = 500000.0 ** (-(jnp.arange(half).astype(jnp.float32) * 2.0) / HD)
    angle = positions.astype(jnp.float32)[:, None] * freqs[None, :]
    cosine = jnp.cos(angle)[:, None, :]
    sine = jnp.sin(angle)[:, None, :]
    parts = value.reshape(rows, heads, HD)
    first = parts[:, :, :half]
    second = parts[:, :, half:]
    out = jnp.concatenate([first * cosine - second * sine, second * cosine + first * sine], axis=2)
    return out.reshape(rows, heads * HD)


def encode_pairs(joined, positions):
    width = KVH * HD
    keys = rope(joined[:, :width], positions, KVH)
    return jnp.concatenate([keys, joined[:, width:]], axis=1).astype(jnp.bfloat16)


def attend(query_head, key_head, value_head, allowed):
    score = jnp.einsum(
        "qd,kd->qk", query_head, key_head, preferred_element_type=jnp.float32
    ) / jnp.sqrt(jnp.float32(HD))
    score = jnp.where(allowed, score, -1e30)
    probs = jax.nn.softmax(score, axis=1).astype(jnp.bfloat16)
    return jnp.dot(probs, value_head, preferred_element_type=jnp.float32).astype(jnp.bfloat16)


def general(x_coded, x_scales, signs, block_order, norm_gain, w_query, w_key, w_value, w_out):
    count = lax.axis_size("tensor")
    index = lax.axis_index("tensor")
    mat = hadamard(BLK)
    sgn = (2 * signs - 1).astype(jnp.float32)
    coded_all, scales_all = (
        lax.all_gather(x_coded, "tensor", axis=1, tiled=True),
        lax.all_gather(x_scales, "tensor", axis=0, tiled=True),
    )
    tokens = coded_all.shape[0]
    nblocks = scales_all.shape[0]
    deq = (
        coded_all.astype(jnp.float32).reshape(tokens, nblocks, BLK)
        * scales_all.astype(jnp.float32).T[:, :, None]
    )
    resid = unrotate_rows(deq.reshape(tokens, -1), sgn, mat)
    inv = lax.rsqrt(jnp.mean(resid * resid, axis=1, keepdims=True) + 1e-05)
    normed = (resid * norm_gain.astype(jnp.float32) * inv).astype(jnp.bfloat16)
    rows = jnp.arange(tokens)
    blen = tokens // NBLOCK
    positions = block_order[rows // blen] * blen + rows % blen
    heads_here = w_query.shape[1] // HD
    query = rope(
        jnp.dot(normed, w_query, preferred_element_type=jnp.float32), positions, heads_here
    ).astype(jnp.bfloat16)
    width = w_key.shape[0]
    mine = lax.dynamic_slice_in_dim(normed, index * width, width, 1)
    joined_w = jnp.concatenate([w_key, w_value], axis=1)
    kv_part = jnp.dot(mine, joined_w, preferred_element_type=jnp.float32)
    share = lax.psum_scatter(kv_part, "tensor", scatter_dimension=0, tiled=True)
    share_rows = share.shape[0]
    share_pos = lax.dynamic_slice_in_dim(positions, index * share_rows, share_rows, 0)
    keyval = lax.all_gather(encode_pairs(share, share_pos), "tensor", axis=0, tiled=True)
    allowed = positions[None, :] <= positions[:, None]
    per_kv = heads_here * count // KVH
    head = index * heads_here + 0
    group = head // per_kv
    key_head = lax.dynamic_slice_in_dim(keyval, group * HD, HD, 1)
    value_head = lax.dynamic_slice_in_dim(keyval, KVH * HD + group * HD, HD, 1)
    outputs = attend(query, key_head, value_head, allowed)
    rotated_w = rotate_rows(w_out.astype(jnp.float32), sgn, mat)
    rotated = jnp.dot(outputs.astype(jnp.float32), rotated_w, precision=HIGH)
    blocks = rotated.reshape(tokens, nblocks, BLK)
    scale = (jnp.max(jnp.abs(blocks), axis=2) + 1e-06).astype(jnp.bfloat16)
    coded = (blocks / scale.astype(jnp.float32)[:, :, None]).astype(jnp.bfloat16)
    send_vals = coded.reshape(tokens, count, width)
    send_scale = scale.reshape(tokens, count, nblocks // count)
    got_vals, got_scale = (
        lax.all_to_all(send_vals, "tensor", split_axis=1, concat_axis=1, tiled=True),
        lax.all_to_all(send_scale, "tensor", split_axis=1, concat_axis=1, tiled=True),
    )
    back = (
        got_vals.astype(jnp.float32).reshape(tokens, count, width // BLK, BLK)
        * got_scale.astype(jnp.float32)[:, :, :, None]
    )
    summed = jnp.sum(back, axis=1).reshape(tokens, width)
    sgn_mine = lax.dynamic_slice_in_dim(sgn, index * width, width, 0)
    resid_mine = lax.dynamic_slice_in_dim(resid, index * width, width, 1)
    newres = resid_mine + unrotate_rows(summed, sgn_mine, mat)
    final = rotate_rows(newres, sgn_mine, mat).reshape(tokens, width // BLK, BLK)
    out_scale = (jnp.max(jnp.abs(final), axis=2) + 1e-06).astype(jnp.bfloat16)
    out_coded = (final / out_scale.astype(jnp.float32)[:, :, None]).astype(jnp.bfloat16)
    return (out_coded.reshape(tokens, width), out_scale.T)


def spin(rows, cols):
    i = lax.broadcasted_iota(jnp.int32, (rows, cols), 0)
    j = lax.broadcasted_iota(jnp.int32, (rows, cols), 1)
    v = i & j
    v = v ^ (v >> 4)
    v = v ^ (v >> 2)
    v = v ^ (v >> 1)
    return (1 - 2 * (v & 1)).astype(jnp.float32).astype(jnp.bfloat16)


def dot(a, b):
    return jnp.dot(a, b, preferred_element_type=jnp.float32)


VMEM = pl.BlockSpec(memory_space=pltpu.VMEM)
SMEM = pl.BlockSpec(memory_space=pltpu.SMEM)
HBM = pl.BlockSpec(memory_space=pltpu.HBM)
ANY = pl.BlockSpec(memory_space=pl.ANY)


def call(kernel, outs, args, specs, scratch=(), micros=1):
    many = isinstance(outs, tuple)
    args = [pltpu.with_memory_space_constraint(a, pltpu.HBM) if spec is HBM else a for a, spec in zip(args, specs)]
    return pl.pallas_call(
        kernel,
        out_shape=outs,
        in_specs=specs,
        out_specs=(VMEM,) * len(outs) if many else VMEM,
        scratch_shapes=scratch,
        compiler_params=pltpu.CompilerParams(vmem_limit_bytes=32 * 2**20),
        cost_estimate=pl.CostEstimate(flops=micros * 10**9, bytes_accessed=10**6, transcendentals=0),
    )(*args)


def fetch(pairs, sems):
    copies = [pltpu.make_async_copy(src, dst, sems.at[k]) for k, (src, dst) in enumerate(pairs)]
    for copy in copies:
        copy.start()
    return copies


def unrotate_kernel(
    me, x_hbm, s_hbm, sign_hbm, gain_hbm, u_ref, x, s, sign, gain, held, sems
):
    per = sign.shape[0]
    at = pl.multiple_of(me[0] * per, per)
    copies = fetch(
        ((gain_hbm, gain), (sign_hbm.at[pl.ds(at, per), :], sign), (s_hbm, s), (x_hbm, x)),
        sems,
    )

    had = spin(BLK, BLK)
    copies[0].wait()
    held[...] = gain[...].astype(jnp.float32)
    copies[1].wait()
    sg = held[pl.ds(at, per), :] * ((2 * sign[...] - 1).astype(jnp.float32) / math.sqrt(BLK))
    copies[2].wait()
    scale = s[...].astype(jnp.float32).T
    copies[3].wait()
    tokens = x.shape[0]
    stacked = jnp.concatenate([x[:, b * BLK : (b + 1) * BLK] for b in range(per)], axis=0)
    turned = dot(stacked, had)
    for b in range(per):
        part = turned[b * tokens : (b + 1) * tokens] * scale[:, b : b + 1]
        u_ref[:, b * BLK : (b + 1) * BLK] = (part * sg[b : b + 1, :]).astype(jnp.bfloat16)


def token_kernel(*refs):
    refs[-1][...] = jnp.zeros_like(refs[-1])


def keyval_kernel(me, u_ref, wk_hbm, wv_hbm, kv_ref, first, second, sems):
    copies = fetch(((wk_hbm, first), (wv_hbm, second)), sems)
    core, chip = me[0] & 1, me[0] >> 1
    for kind, weights in enumerate((first, second)):
        copies[kind].wait()
        part = dot(u_ref[...], weights[...]).astype(jnp.bfloat16)
        for p in range(KVH):
            kv_ref[1 - (core ^ kind), (chip ^ p) & 1, p >> 1] = part[:, p * HD : (p + 1) * HD]


def joint(me, w_hbm, x_hbm, rel, into):
    width = into.shape[0]
    at = pl.ds(pl.multiple_of((me[0] ^ rel) * width, width), width)
    return [(w_hbm.at[at, :], into.at[:, pl.ds(0, HD)]), (x_hbm.at[at, :], into.at[:, pl.ds(HD, HD)])]


def products(me, rel, u, weights, held):
    per = u.shape[1] // BLK
    inverse = held[pl.ds(pl.multiple_of((me[0] ^ rel) * per, per), per), :]
    square = 0.0
    for b in range(per):
        r = u[:, b * BLK : (b + 1) * BLK].astype(jnp.float32) * inverse[b : b + 1, :]
        square = square + r * r
    return dot(u, weights), square


def query_kernel(rels, me, token, gain_ref, w_hbm, x_hbm, *refs):
    n = len(rels)
    us, (pay_ref, ws, held, sems) = refs[:n], refs[n:]
    pairs = []
    for k, rel in enumerate(rels):
        pairs += joint(me, w_hbm, x_hbm, rel, ws.at[k])
    copies = fetch(pairs, sems)
    held[...] = 1.0 / gain_ref[...].astype(jnp.float32)
    pay, square = 0.0, 0.0
    for k, rel in enumerate(rels):
        copies[2 * k].wait()
        copies[2 * k + 1].wait()
        part, squares = products(me, rel, us[k][...], ws[k], held)
        pay, square = pay + part, square + squares
    pay_ref[:, : 2 * HD] = pay
    pay_ref[:, 2 * HD :] = square


def more_kernel(rels, ahead, me, done, gain_ref, w_hbm, x_hbm, before_ref, *refs):
    n = len(rels)
    us, (pay_ref, ahead_ref, ws, held, sems) = refs[:n], refs[n:]
    pairs = []
    for k, rel in enumerate(rels):
        pairs += joint(me, w_hbm, x_hbm, rel, ws.at[k])
    for k, rel in enumerate(ahead):
        pairs += joint(me, w_hbm, x_hbm, rel, ahead_ref.at[k])
    copies = fetch(pairs, sems)
    held[...] = 1.0 / gain_ref[...].astype(jnp.float32)
    pay, square = before_ref[:, : 2 * HD], before_ref[:, 2 * HD :]
    for k, rel in enumerate(rels):
        copies[2 * k].wait()
        copies[2 * k + 1].wait()
        part, squares = products(me, rel, us[k][...], ws[k], held)
        pay, square = pay + part, square + squares
    for copy in copies[2 * n :]:
        copy.wait()
    pay_ref[:, : 2 * HD] = pay
    pay_ref[:, 2 * HD :] = square


def last_kernel(rels, me, done, gain_ref, w_ref, before_ref, *refs):
    us, (pay_ref, held) = refs[:-2], refs[-2:]
    held[...] = 1.0 / gain_ref[...].astype(jnp.float32)
    pay, square = before_ref[:, : 2 * HD], before_ref[:, 2 * HD :]
    for k, rel in enumerate(rels):
        part, squares = products(me, rel, us[k][...], w_ref[k], held)
        pay, square = pay + part, square + squares
    pay_ref[:, : 2 * HD] = pay
    pay_ref[:, 2 * HD :] = square


def turn(value, cosine, sine):
    half = HD // 2
    swapped = jnp.concatenate([value[:, half:], value[:, :half]], axis=1)
    return (value * cosine + swapped * sine).astype(jnp.bfloat16)


def columns(me, rel, width):
    return pl.ds(pl.multiple_of((me[0] ^ rel) * width, width), width)


def put(outs, value):
    at = 0
    while at < value.shape[0]:
        rows = outs[0].shape[0]
        outs[0][...] = value[at : at + rows].astype(outs[0].dtype)
        at, outs = at + rows, outs[1:]
    return outs


def attend_kernel(total, rels, me, pay_ref, got_ref, kv_ref, kvx_ref, cos_ref, sin_ref, row_ref, col_ref, w_hbm, x_hbm, *refs):
    att_ref, outs, (ws, xs, sems) = refs[0], refs[1:-3], refs[-3:]
    width = ws.shape[2]
    copies = fetch(
        [(src.at[:, columns(me, rel, width)], dst.at[k]) for k, rel in enumerate(rels) for src, dst in ((w_hbm, ws), (x_hbm, xs))],
        sems,
    )
    square = jnp.sum(pay_ref[:, 2 * HD :] + got_ref[:, 2 * HD :], axis=1, keepdims=True)
    inv = lax.rsqrt(square / total + 1e-05)
    cosine, sine = cos_ref[...], sin_ref[...]
    core = me[0] & 1
    mine, theirs = kv_ref[...].astype(jnp.float32), kvx_ref[...].astype(jnp.float32)
    key = turn(jnp.where(core == 0, mine, theirs) * inv, cosine, sine)
    value = (jnp.where(core == 0, theirs, mine) * inv).astype(jnp.bfloat16)
    allowed = row_ref[...] <= col_ref[...]
    heads = []
    for at in range(2):
        query = pay_ref[:, at * HD : (at + 1) * HD] + got_ref[:, (1 - at) * HD : (2 - at) * HD]
        query = turn(query * inv, cosine, sine)
        score = lax.dot_general(query, key, (((1,), (1,)), ((), ())), preferred_element_type=jnp.float32)
        score = jnp.where(allowed, score / math.sqrt(HD), -1e30)
        weight = jnp.exp(score - jnp.max(score, axis=1, keepdims=True))
        probs = (weight / jnp.sum(weight, axis=1, keepdims=True)).astype(jnp.bfloat16)
        head = dot(probs, value).astype(jnp.bfloat16)
        att_ref[:, at * HD : (at + 1) * HD] = head
        heads.append(head)
    for k in range(len(rels)):
        copies[2 * k].wait()
        copies[2 * k + 1].wait()
        outs = put(outs, dot(heads[0], ws[k]) + dot(heads[1], xs[k]))


def term_kernel(rels, me, att_ref, w_hbm, x_hbm, *refs):
    outs, (ws, xs, sems) = refs[:-3], refs[-3:]
    width = ws.shape[2]
    copies = fetch(
        [(src.at[:, columns(me, rel, width)], dst.at[k]) for k, rel in enumerate(rels) for src, dst in ((w_hbm, ws), (x_hbm, xs))],
        sems,
    )
    for k in range(len(rels)):
        copies[2 * k].wait()
        copies[2 * k + 1].wait()
        outs = put(outs, dot(att_ref[:, :HD], ws[k]) + dot(att_ref[:, HD:], xs[k]))


def final_kernel(n, me, done, x_ref, s_ref, sign_ref, *refs):
    had = spin(BLK, BLK)
    scale = s_ref[...].astype(jnp.float32).T
    per = s_ref.shape[0]
    sign = (2 * sign_ref[pl.ds(pl.multiple_of(me[0] * per, per), per), :] - 1).astype(jnp.float32) / math.sqrt(BLK)
    parts, (coded_ref, scales_ref) = refs[:n], refs[n:]
    tokens = x_ref.shape[0]

    def piece(at):
        held, total = [], 0.0
        for ref in parts:
            held.append(ref[:, at].astype(jnp.float32))
            if sum(h.shape[0] for h in held) == tokens:
                total, held = total + jnp.concatenate(held, axis=0), []
        return total

    sums = jnp.concatenate([piece(slice(b * BLK, (b + 1) * BLK)) * sign[b : b + 1, :] for b in range(per)], axis=0)
    high = sums.astype(jnp.bfloat16)
    rest = sums - high.astype(jnp.float32)
    mid = rest.astype(jnp.bfloat16)
    low = (rest - mid.astype(jnp.float32)).astype(jnp.bfloat16)
    turned = dot(high, had) + (dot(mid, had) + dot(low, had))
    tops = []
    for b in range(per):
        at = slice(b * BLK, (b + 1) * BLK)
        new = turned[b * tokens : (b + 1) * tokens] + x_ref[:, at].astype(jnp.float32) * scale[:, b : b + 1]
        top = (jnp.max(jnp.abs(new), axis=1, keepdims=True) + 1e-06).astype(jnp.bfloat16).astype(jnp.float32)
        coded_ref[:, at] = (new / top).astype(jnp.bfloat16)
        tops.append(top)
    scales_ref[...] = jnp.concatenate(tops, axis=1).T.astype(jnp.bfloat16)


def swap(value, rel):
    count = lax.axis_size("tensor")
    return lax.ppermute(value, "tensor", [(i, i ^ rel) for i in range(count)])


CORE, ACROSS, NEAR, FAR = 1, 2, 4, 8


def paired(x_coded, x_scales, signs, block_order, norm_gain, w_query, w_key, w_value, w_out):
    count = lax.axis_size("tensor")
    index = lax.axis_index("tensor")
    me = jnp.reshape(index, (1,)).astype(jnp.int32)
    tokens, width = x_coded.shape
    bf16, f32 = jnp.bfloat16, jnp.float32
    block = jax.ShapeDtypeStruct((tokens, width), bf16)
    wide = jax.ShapeDtypeStruct((tokens, width), f32)
    half_block = jax.ShapeDtypeStruct((tokens // 2, width), bf16)
    half_wide = jax.ShapeDtypeStruct((tokens // 2, width), f32)
    partial = jax.ShapeDtypeStruct((tokens, 3 * HD), f32)
    dma = pltpu.SemaphoreType.DMA
    together = lax.optimization_barrier
    sign2 = signs.reshape(-1, BLK)
    gain2 = norm_gain.reshape(-1, BLK)

    def plus(*parts):
        return sum(p.astype(f32) for p in parts).astype(bf16)

    def after(*arrays, micros=3):
        return call(token_kernel, jax.ShapeDtypeStruct((8, BLK), f32), arrays, [ANY] * len(arrays), micros=micros)

    u = call(
        unrotate_kernel,
        block,
        (me, x_coded, x_scales, sign2, gain2),
        [SMEM] + [HBM] * 4,
        [
            pltpu.VMEM(x_coded.shape, bf16),
            pltpu.VMEM(x_scales.shape, bf16),
            pltpu.VMEM((width // BLK, BLK), jnp.int32),
            pltpu.VMEM(gain2.shape, bf16),
            pltpu.VMEM(gain2.shape, f32),
            dma((4,)),
        ],
    )

    _, w_query_now = together((u, w_query))
    wq_other = swap(w_query_now, CORE)
    kv = call(
        keyval_kernel,
        jax.ShapeDtypeStruct((2, 2, KVH // 2, tokens, HD), bf16),
        (me, u, w_key, w_value),
        [SMEM, VMEM, HBM, HBM],
        [pltpu.VMEM(w_key.shape, bf16), pltpu.VMEM(w_key.shape, bf16), dma((2,))],
        micros=20,
    )
    kv = plus(kv[1], swap(kv[0], CORE))
    kv_across = swap(kv[1], ACROSS)
    far = swap(u, FAR)
    across = swap(u, ACROSS)
    near = swap(u, NEAR)
    w_out_now = w_out
    done = after(after(across, near, micros=10), far, micros=30)
    near, kv_across, across, wq_other, far, w_out_now, done = together(
        (near, kv_across, across, wq_other, far, w_out_now, done)
    )
    chunk = {0: u, 2: across, 4: near, 8: far}
    kv = plus(kv[0], kv_across)

    early, more, late = (0, 2, 4), (8, 10, 12), (6, 14)
    pay = call(
        functools.partial(query_kernel, early),
        partial,
        (me, done, gain2, w_query, wq_other) + tuple(chunk[rel] for rel in early),
        [SMEM, ANY, VMEM, HBM, HBM] + [VMEM] * len(early),
        [
            pltpu.VMEM((len(early), width, 2 * HD), bf16),
            pltpu.VMEM(gain2.shape, f32),
            dma((2 * len(early),)),
        ],
        micros=10,
    )
    wo_other = swap(w_out_now, CORE)
    chunk[12] = swap(chunk[8], NEAR)
    chunk[10] = swap(chunk[8], ACROSS)
    pay, kv = together((pay, kv))
    alike = [[4 * z + low for z in range(count // 4)] for low in range(4)]
    kv = lax.all_to_all(kv, "tensor", 0, 0, axis_index_groups=alike, tiled=True)
    done = after(chunk[12], chunk[10])
    done, chunk[2], chunk[12], chunk[10], pay, _ = together((done, chunk[2], chunk[12], chunk[10], pay, w_out_now))

    chunk[14] = swap(chunk[12], ACROSS)
    chunk[6] = swap(chunk[2], NEAR)
    pay, ahead = call(
        functools.partial(more_kernel, more, late),
        (partial, jax.ShapeDtypeStruct((len(late), width, 2 * HD), bf16)),
        (me, done, gain2, w_query, wq_other, pay) + tuple(chunk[rel] for rel in more),
        [SMEM, ANY, VMEM, HBM, HBM, VMEM] + [VMEM] * len(more),
        [
            pltpu.VMEM((len(more), width, 2 * HD), bf16),
            pltpu.VMEM(gain2.shape, f32),
            dma((2 * len(more + late),)),
        ],
        micros=20,
    )
    kv = jnp.sum(kv.astype(f32), axis=0).astype(bf16)
    kv_other = swap(kv, CORE)
    pay = call(
        functools.partial(last_kernel, late),
        partial,
        (me, after(chunk[14], chunk[6], micros=10), gain2, ahead, pay) + tuple(chunk[rel] for rel in late),
        [SMEM, ANY] + [VMEM] * (3 + len(late)),
        [pltpu.VMEM(gain2.shape, f32)],
    )
    got = swap(pay, CORE)

    blen = tokens // NBLOCK
    positions = (block_order[:, None] * blen + jnp.arange(blen)[None, :]).reshape(-1)
    half = HD // 2
    freqs = 500000.0 ** (-(jnp.arange(half).astype(f32) * 2.0) / HD)
    angle = positions.astype(f32)[:, None] * freqs[None, :]
    cosine, sine = jnp.cos(angle), jnp.sin(angle)
    cosine = jnp.concatenate([cosine, cosine], axis=1)
    sine = jnp.concatenate([-sine, sine], axis=1)

    def buffers(n):
        return [pltpu.VMEM((n, HD, width), bf16), pltpu.VMEM((n, HD, width), bf16), dma((2 * n,))]

    args = (me, pay, got, kv, kv_other, cosine, sine, positions[None, :], positions[:, None], w_out, wo_other)
    att, t14a, t14b = call(
        functools.partial(attend_kernel, count * width, (14,)),
        (jax.ShapeDtypeStruct((tokens, 2 * HD), bf16), half_block, half_block),
        args,
        [SMEM] + [VMEM] * 8 + [HBM] * 2,
        buffers(1),
    )

    x14a = swap(t14a, ACROSS)
    rels = (10, 6, 2, 12, 8, 4, 0)
    t10a, t10b, t6a, t6b, t2, t12a, t12b, t8a, t8b, t4a, t4b, t0 = call(
        functools.partial(term_kernel, rels),
        (half_block,) * 4 + (block,) + (half_wide,) * 6 + (wide,),
        (me, att, w_out, wo_other),
        [SMEM, VMEM, HBM, HBM],
        buffers(len(rels)),
        micros=20,
    )
    x14b = swap(t14b, ACROSS)
    x14a, t10a = together((x14a, t10a))
    n12a = swap(plus(t12a, x14a), NEAR)
    x10a = swap(t10a, ACROSS)
    x14b, t10b = together((x14b, t10b))
    n12b = swap(plus(t12b, x14b), NEAR)
    x10b = swap(t10b, ACROSS)
    n12a, x10a, t6a = together((n12a, x10a, t6a))
    n8a = swap(plus(t8a, x10a, n12a), FAR)
    x6a = swap(t6a, ACROSS)
    n12b, x10b, t6b = together((n12b, x10b, t6b))
    n8b = swap(plus(t8b, x10b, n12b), FAR)
    x6b = swap(t6b, ACROSS)
    _, t2 = together((x10b, t2))
    n4a = swap(plus(t4a, x6a), NEAR)
    n4b = swap(plus(t4b, x6b), NEAR)
    x2 = swap(t2, ACROSS)
    parts = (t0, x2, n4a, n4b, n8a, n8b)
    return call(
        functools.partial(final_kernel, len(parts)),
        (block, jax.ShapeDtypeStruct(x_scales.shape, bf16)),
        (me, after(n8b), x_coded, x_scales, sign2) + parts,
        [SMEM, ANY] + [VMEM] * (3 + len(parts)),
    )


def per_device(*args):
    if lax.axis_size("tensor") == 16:
        return paired(*args)
    return general(*args)


def solution(mesh):
    in_specs = (
        P("group", "tensor"),
        P("tensor", "group"),
        P(),
        P("group"),
        P(),
        P(None, "tensor"),
        P("tensor", None),
        P("tensor", None),
        P("tensor", None),
    )
    out_specs = (P("group", "tensor"), P("tensor", "group"))
    return jax.shard_map(
        per_device, mesh=mesh, in_specs=in_specs, out_specs=out_specs, check_vma=False
    )
```

```python
import functools
import math

import jax
import jax.numpy as jnp
from jax import lax
from jax.experimental import pallas as pl
from jax.experimental.pallas import tpu as pltpu
from jax.sharding import PartitionSpec as P

HD = 128
KVH = 8
BLK = 128
NBLOCK = 16


HIGH = lax.Precision.HIGHEST


def hadamard(width):
    idx = jnp.arange(width)
    parity = jnp.zeros((width, width), jnp.int32)
    bit = 1
    while bit < width:
        parity = parity + idx[:, None] // bit % 2 * (idx[None, :] // bit % 2)
        bit = bit * 2
    return jnp.where(parity % 2 == 0, 1.0, -1.0).astype(jnp.float32) / jnp.sqrt(jnp.float32(width))


def rotate_rows(value, sgn, mat):
    rows = value.shape[0]
    blocks = (value * sgn).reshape(rows, -1, mat.shape[0])
    return jnp.einsum("tnb,bc->tnc", blocks, mat, precision=HIGH).reshape(rows, -1)


def unrotate_rows(value, sgn, mat):
    rows = value.shape[0]
    blocks = value.reshape(rows, -1, mat.shape[0])
    return jnp.einsum("tnb,bc->tnc", blocks, mat, precision=HIGH).reshape(rows, -1) * sgn


def rope(value, positions, heads):
    rows = value.shape[0]
    half = HD // 2
    freqs = 500000.0 ** (-(jnp.arange(half).astype(jnp.float32) * 2.0) / HD)
    angle = positions.astype(jnp.float32)[:, None] * freqs[None, :]
    cosine = jnp.cos(angle)[:, None, :]
    sine = jnp.sin(angle)[:, None, :]
    parts = value.reshape(rows, heads, HD)
    first = parts[:, :, :half]
    second = parts[:, :, half:]
    out = jnp.concatenate([first * cosine - second * sine, second * cosine + first * sine], axis=2)
    return out.reshape(rows, heads * HD)


def encode_pairs(joined, positions):
    width = KVH * HD
    keys = rope(joined[:, :width], positions, KVH)
    return jnp.concatenate([keys, joined[:, width:]], axis=1).astype(jnp.bfloat16)


def attend(query_head, key_head, value_head, allowed):
    score = jnp.einsum(
        "qd,kd->qk", query_head, key_head, preferred_element_type=jnp.float32
    ) / jnp.sqrt(jnp.float32(HD))
    score = jnp.where(allowed, score, -1e30)
    probs = jax.nn.softmax(score, axis=1).astype(jnp.bfloat16)
    return jnp.dot(probs, value_head, preferred_element_type=jnp.float32).astype(jnp.bfloat16)


def general(x_coded, x_scales, signs, block_order, norm_gain, w_query, w_key, w_value, w_out):
    count = lax.axis_size("tensor")
    index = lax.axis_index("tensor")
    mat = hadamard(BLK)
    sgn = (2 * signs - 1).astype(jnp.float32)
    coded_all, scales_all = (
        lax.all_gather(x_coded, "tensor", axis=1, tiled=True),
        lax.all_gather(x_scales, "tensor", axis=0, tiled=True),
    )
    tokens = coded_all.shape[0]
    nblocks = scales_all.shape[0]
    deq = (
        coded_all.astype(jnp.float32).reshape(tokens, nblocks, BLK)
        * scales_all.astype(jnp.float32).T[:, :, None]
    )
    resid = unrotate_rows(deq.reshape(tokens, -1), sgn, mat)
    inv = lax.rsqrt(jnp.mean(resid * resid, axis=1, keepdims=True) + 1e-05)
    normed = (resid * norm_gain.astype(jnp.float32) * inv).astype(jnp.bfloat16)
    rows = jnp.arange(tokens)
    blen = tokens // NBLOCK
    positions = block_order[rows // blen] * blen + rows % blen
    heads_here = w_query.shape[1] // HD
    query = rope(
        jnp.dot(normed, w_query, preferred_element_type=jnp.float32), positions, heads_here
    ).astype(jnp.bfloat16)
    width = w_key.shape[0]
    mine = lax.dynamic_slice_in_dim(normed, index * width, width, 1)
    joined_w = jnp.concatenate([w_key, w_value], axis=1)
    kv_part = jnp.dot(mine, joined_w, preferred_element_type=jnp.float32)
    share = lax.psum_scatter(kv_part, "tensor", scatter_dimension=0, tiled=True)
    share_rows = share.shape[0]
    share_pos = lax.dynamic_slice_in_dim(positions, index * share_rows, share_rows, 0)
    keyval = lax.all_gather(encode_pairs(share, share_pos), "tensor", axis=0, tiled=True)
    allowed = positions[None, :] <= positions[:, None]
    per_kv = heads_here * count // KVH
    head = index * heads_here + 0
    group = head // per_kv
    key_head = lax.dynamic_slice_in_dim(keyval, group * HD, HD, 1)
    value_head = lax.dynamic_slice_in_dim(keyval, KVH * HD + group * HD, HD, 1)
    outputs = attend(query, key_head, value_head, allowed)
    rotated_w = rotate_rows(w_out.astype(jnp.float32), sgn, mat)
    rotated = jnp.dot(outputs.astype(jnp.float32), rotated_w, precision=HIGH)
    blocks = rotated.reshape(tokens, nblocks, BLK)
    scale = (jnp.max(jnp.abs(blocks), axis=2) + 1e-06).astype(jnp.bfloat16)
    coded = (blocks / scale.astype(jnp.float32)[:, :, None]).astype(jnp.bfloat16)
    send_vals = coded.reshape(tokens, count, width)
    send_scale = scale.reshape(tokens, count, nblocks // count)
    got_vals, got_scale = (
        lax.all_to_all(send_vals, "tensor", split_axis=1, concat_axis=1, tiled=True),
        lax.all_to_all(send_scale, "tensor", split_axis=1, concat_axis=1, tiled=True),
    )
    back = (
        got_vals.astype(jnp.float32).reshape(tokens, count, width // BLK, BLK)
        * got_scale.astype(jnp.float32)[:, :, :, None]
    )
    summed = jnp.sum(back, axis=1).reshape(tokens, width)
    sgn_mine = lax.dynamic_slice_in_dim(sgn, index * width, width, 0)
    resid_mine = lax.dynamic_slice_in_dim(resid, index * width, width, 1)
    newres = resid_mine + unrotate_rows(summed, sgn_mine, mat)
    final = rotate_rows(newres, sgn_mine, mat).reshape(tokens, width // BLK, BLK)
    out_scale = (jnp.max(jnp.abs(final), axis=2) + 1e-06).astype(jnp.bfloat16)
    out_coded = (final / out_scale.astype(jnp.float32)[:, :, None]).astype(jnp.bfloat16)
    return (out_coded.reshape(tokens, width), out_scale.T)


def spin(rows, cols):
    i = lax.broadcasted_iota(jnp.int32, (rows, cols), 0)
    j = lax.broadcasted_iota(jnp.int32, (rows, cols), 1)
    v = i & j
    v = v ^ (v >> 4)
    v = v ^ (v >> 2)
    v = v ^ (v >> 1)
    return (1 - 2 * (v & 1)).astype(jnp.float32).astype(jnp.bfloat16)


def dot(a, b):
    return jnp.dot(a, b, preferred_element_type=jnp.float32)


VMEM = pl.BlockSpec(memory_space=pltpu.VMEM)
SMEM = pl.BlockSpec(memory_space=pltpu.SMEM)
HBM = pl.BlockSpec(memory_space=pltpu.HBM)
ANY = pl.BlockSpec(memory_space=pl.ANY)


def call(kernel, outs, args, specs, scratch=(), micros=1):
    many = isinstance(outs, tuple)
    args = [pltpu.with_memory_space_constraint(a, pltpu.HBM) if spec is HBM else a for a, spec in zip(args, specs)]
    return pl.pallas_call(
        kernel,
        out_shape=outs,
        in_specs=specs,
        out_specs=(VMEM,) * len(outs) if many else VMEM,
        scratch_shapes=scratch,
        compiler_params=pltpu.CompilerParams(vmem_limit_bytes=32 * 2**20),
        cost_estimate=pl.CostEstimate(flops=micros * 10**9, bytes_accessed=10**6, transcendentals=0),
    )(*args)


def fetch(pairs, sems):
    copies = [pltpu.make_async_copy(src, dst, sems.at[k]) for k, (src, dst) in enumerate(pairs)]
    for copy in copies:
        copy.start()
    return copies


def unrotate_kernel(
    me, x_hbm, s_hbm, sign_hbm, gain_hbm, u_ref, x, s, sign, gain, held, sems
):
    per = sign.shape[0]
    at = pl.multiple_of(me[0] * per, per)
    copies = fetch(
        ((gain_hbm, gain), (sign_hbm.at[pl.ds(at, per), :], sign), (s_hbm, s), (x_hbm, x)),
        sems,
    )

    had = spin(BLK, BLK)
    copies[0].wait()
    held[...] = gain[...].astype(jnp.float32)
    copies[1].wait()
    sg = held[pl.ds(at, per), :] * ((2 * sign[...] - 1).astype(jnp.float32) / math.sqrt(BLK))
    copies[2].wait()
    scale = s[...].astype(jnp.float32).T
    copies[3].wait()
    tokens = x.shape[0]
    stacked = jnp.concatenate([x[:, b * BLK : (b + 1) * BLK] for b in range(per)], axis=0)
    turned = dot(stacked, had)
    for b in range(per):
        part = turned[b * tokens : (b + 1) * tokens] * scale[:, b : b + 1]
        u_ref[:, b * BLK : (b + 1) * BLK] = (part * sg[b : b + 1, :]).astype(jnp.bfloat16)


def token_kernel(*refs):
    refs[-1][...] = jnp.zeros_like(refs[-1])


def keyval_kernel(me, u_ref, wk_hbm, wv_hbm, kv_ref, first, second, sems):
    copies = fetch(((wk_hbm, first), (wv_hbm, second)), sems)
    core, chip = me[0] & 1, me[0] >> 1
    for kind, weights in enumerate((first, second)):
        copies[kind].wait()
        part = dot(u_ref[...], weights[...]).astype(jnp.bfloat16)
        for p in range(KVH):
            kv_ref[1 - (core ^ kind), (chip ^ p) & 1, p >> 1] = part[:, p * HD : (p + 1) * HD]


def joint(me, w_hbm, x_hbm, rel, into):
    width = into.shape[0]
    at = pl.ds(pl.multiple_of((me[0] ^ rel) * width, width), width)
    return [(w_hbm.at[at, :], into.at[:, pl.ds(0, HD)]), (x_hbm.at[at, :], into.at[:, pl.ds(HD, HD)])]


def products(me, rel, u, weights, held):
    per = u.shape[1] // BLK
    inverse = held[pl.ds(pl.multiple_of((me[0] ^ rel) * per, per), per), :]
    square = 0.0
    for b in range(per):
        r = u[:, b * BLK : (b + 1) * BLK].astype(jnp.float32) * inverse[b : b + 1, :]
        square = square + r * r
    return dot(u, weights), square


def query_kernel(rels, me, token, gain_ref, w_hbm, x_hbm, *refs):
    n = len(rels)
    us, (pay_ref, ws, held, sems) = refs[:n], refs[n:]
    pairs = []
    for k, rel in enumerate(rels):
        pairs += joint(me, w_hbm, x_hbm, rel, ws.at[k])
    copies = fetch(pairs, sems)
    held[...] = 1.0 / gain_ref[...].astype(jnp.float32)
    pay, square = 0.0, 0.0
    for k, rel in enumerate(rels):
        copies[2 * k].wait()
        copies[2 * k + 1].wait()
        part, squares = products(me, rel, us[k][...], ws[k], held)
        pay, square = pay + part, square + squares
    pay_ref[:, : 2 * HD] = pay
    pay_ref[:, 2 * HD :] = square


def more_kernel(rels, ahead, me, done, gain_ref, w_hbm, x_hbm, before_ref, *refs):
    n = len(rels)
    us, (pay_ref, ahead_ref, ws, held, sems) = refs[:n], refs[n:]
    pairs = []
    for k, rel in enumerate(rels):
        pairs += joint(me, w_hbm, x_hbm, rel, ws.at[k])
    for k, rel in enumerate(ahead):
        pairs += joint(me, w_hbm, x_hbm, rel, ahead_ref.at[k])
    copies = fetch(pairs, sems)
    held[...] = 1.0 / gain_ref[...].astype(jnp.float32)
    pay, square = before_ref[:, : 2 * HD], before_ref[:, 2 * HD :]
    for k, rel in enumerate(rels):
        copies[2 * k].wait()
        copies[2 * k + 1].wait()
        part, squares = products(me, rel, us[k][...], ws[k], held)
        pay, square = pay + part, square + squares
    for copy in copies[2 * n :]:
        copy.wait()
    pay_ref[:, : 2 * HD] = pay
    pay_ref[:, 2 * HD :] = square


def last_kernel(rels, me, done, gain_ref, w_ref, before_ref, *refs):
    us, (pay_ref, held) = refs[:-2], refs[-2:]
    held[...] = 1.0 / gain_ref[...].astype(jnp.float32)
    pay, square = before_ref[:, : 2 * HD], before_ref[:, 2 * HD :]
    for k, rel in enumerate(rels):
        part, squares = products(me, rel, us[k][...], w_ref[k], held)
        pay, square = pay + part, square + squares
    pay_ref[:, : 2 * HD] = pay
    pay_ref[:, 2 * HD :] = square


def turn(value, cosine, sine):
    half = HD // 2
    swapped = jnp.concatenate([value[:, half:], value[:, :half]], axis=1)
    return (value * cosine + swapped * sine).astype(jnp.bfloat16)


def columns(me, rel, width):
    return pl.ds(pl.multiple_of((me[0] ^ rel) * width, width), width)


def put(outs, value):
    at = 0
    while at < value.shape[0]:
        rows = outs[0].shape[0]
        outs[0][...] = value[at : at + rows].astype(outs[0].dtype)
        at, outs = at + rows, outs[1:]
    return outs


def attend_kernel(total, rels, me, done, pay_ref, got_ref, kv_ref, kvx_ref, cos_ref, sin_ref, row_ref, col_ref, w_hbm, x_hbm, *refs):
    att_ref, outs, (ws, xs, sems) = refs[0], refs[1:-3], refs[-3:]
    width = ws.shape[2]
    copies = fetch(
        [(src.at[:, columns(me, rel, width)], dst.at[k]) for k, rel in enumerate(rels) for src, dst in ((w_hbm, ws), (x_hbm, xs))],
        sems,
    )
    square = jnp.sum(pay_ref[:, 2 * HD :] + got_ref[:, 2 * HD :], axis=1, keepdims=True)
    inv = lax.rsqrt(square / total + 1e-05)
    cosine, sine = cos_ref[...], sin_ref[...]
    core = me[0] & 1
    mine, theirs = kv_ref[...].astype(jnp.float32), kvx_ref[...].astype(jnp.float32)
    key = turn(jnp.where(core == 0, mine, theirs) * inv, cosine, sine)
    value = (jnp.where(core == 0, theirs, mine) * inv).astype(jnp.bfloat16)
    allowed = row_ref[...] <= col_ref[...]
    heads = []
    for at in range(2):
        query = pay_ref[:, at * HD : (at + 1) * HD] + got_ref[:, (1 - at) * HD : (2 - at) * HD]
        query = turn(query * inv, cosine, sine)
        score = lax.dot_general(query, key, (((1,), (1,)), ((), ())), preferred_element_type=jnp.float32)
        score = jnp.where(allowed, score / math.sqrt(HD), -1e30)
        weight = jnp.exp(score - jnp.max(score, axis=1, keepdims=True))
        probs = (weight / jnp.sum(weight, axis=1, keepdims=True)).astype(jnp.bfloat16)
        head = dot(probs, value).astype(jnp.bfloat16)
        att_ref[:, at * HD : (at + 1) * HD] = head
        heads.append(head)
    for k in range(len(rels)):
        copies[2 * k].wait()
        copies[2 * k + 1].wait()
        outs = put(outs, dot(heads[0], ws[k]) + dot(heads[1], xs[k]))


def term_kernel(rels, me, att_ref, w_hbm, x_hbm, *refs):
    outs, (ws, xs, sems) = refs[:-3], refs[-3:]
    width = ws.shape[2]
    copies = fetch(
        [(src.at[:, columns(me, rel, width)], dst.at[k]) for k, rel in enumerate(rels) for src, dst in ((w_hbm, ws), (x_hbm, xs))],
        sems,
    )
    for k in range(len(rels)):
        copies[2 * k].wait()
        copies[2 * k + 1].wait()
        outs = put(outs, dot(att_ref[:, :HD], ws[k]) + dot(att_ref[:, HD:], xs[k]))


def final_kernel(n, me, done, x_ref, s_ref, sign_ref, *refs):
    had = spin(BLK, BLK)
    scale = s_ref[...].astype(jnp.float32).T
    per = s_ref.shape[0]
    sign = (2 * sign_ref[pl.ds(pl.multiple_of(me[0] * per, per), per), :] - 1).astype(jnp.float32) / math.sqrt(BLK)
    parts, (coded_ref, scales_ref) = refs[:n], refs[n:]
    tokens = x_ref.shape[0]

    def piece(at):
        held, total = [], 0.0
        for ref in parts:
            held.append(ref[:, at].astype(jnp.float32))
            if sum(h.shape[0] for h in held) == tokens:
                total, held = total + jnp.concatenate(held, axis=0), []
        return total

    sums = jnp.concatenate([piece(slice(b * BLK, (b + 1) * BLK)) * sign[b : b + 1, :] for b in range(per)], axis=0)
    high = sums.astype(jnp.bfloat16)
    rest = sums - high.astype(jnp.float32)
    mid = rest.astype(jnp.bfloat16)
    low = (rest - mid.astype(jnp.float32)).astype(jnp.bfloat16)
    turned = dot(high, had) + (dot(mid, had) + dot(low, had))
    tops = []
    for b in range(per):
        at = slice(b * BLK, (b + 1) * BLK)
        new = turned[b * tokens : (b + 1) * tokens] + x_ref[:, at].astype(jnp.float32) * scale[:, b : b + 1]
        top = (jnp.max(jnp.abs(new), axis=1, keepdims=True) + 1e-06).astype(jnp.bfloat16).astype(jnp.float32)
        coded_ref[:, at] = (new / top).astype(jnp.bfloat16)
        tops.append(top)
    scales_ref[...] = jnp.concatenate(tops, axis=1).T.astype(jnp.bfloat16)


def swap(value, rel):
    count = lax.axis_size("tensor")
    return lax.ppermute(value, "tensor", [(i, i ^ rel) for i in range(count)])


CORE, ACROSS, NEAR, FAR = 1, 2, 4, 8


def paired(x_coded, x_scales, signs, block_order, norm_gain, w_query, w_key, w_value, w_out):
    count = lax.axis_size("tensor")
    index = lax.axis_index("tensor")
    me = jnp.reshape(index, (1,)).astype(jnp.int32)
    tokens, width = x_coded.shape
    bf16, f32 = jnp.bfloat16, jnp.float32
    block = jax.ShapeDtypeStruct((tokens, width), bf16)
    wide = jax.ShapeDtypeStruct((tokens, width), f32)
    half_block = jax.ShapeDtypeStruct((tokens // 2, width), bf16)
    half_wide = jax.ShapeDtypeStruct((tokens // 2, width), f32)
    partial = jax.ShapeDtypeStruct((tokens, 3 * HD), f32)
    dma = pltpu.SemaphoreType.DMA
    together = lax.optimization_barrier
    sign2 = signs.reshape(-1, BLK)
    gain2 = norm_gain.reshape(-1, BLK)

    def plus(*parts):
        return sum(p.astype(f32) for p in parts).astype(bf16)

    def after(*arrays, micros=3):
        return call(token_kernel, jax.ShapeDtypeStruct((8, BLK), f32), arrays, [ANY] * len(arrays), micros=micros)

    u = call(
        unrotate_kernel,
        block,
        (me, x_coded, x_scales, sign2, gain2),
        [SMEM] + [HBM] * 4,
        [
            pltpu.VMEM(x_coded.shape, bf16),
            pltpu.VMEM(x_scales.shape, bf16),
            pltpu.VMEM((width // BLK, BLK), jnp.int32),
            pltpu.VMEM(gain2.shape, bf16),
            pltpu.VMEM(gain2.shape, f32),
            dma((4,)),
        ],
    )

    _, w_query_now = together((u, w_query))
    wq_other = swap(w_query_now, CORE)
    kv = call(
        keyval_kernel,
        jax.ShapeDtypeStruct((2, 2, KVH // 2, tokens, HD), bf16),
        (me, u, w_key, w_value),
        [SMEM, VMEM, HBM, HBM],
        [pltpu.VMEM(w_key.shape, bf16), pltpu.VMEM(w_key.shape, bf16), dma((2,))],
        micros=20,
    )
    kv = plus(kv[1], swap(kv[0], CORE))
    kv_across = swap(kv[1], ACROSS)
    far = swap(u, FAR)
    across = swap(u, ACROSS)
    near = swap(u, NEAR)
    w_out_now = w_out
    done = after(after(across, near, micros=10), far, micros=30)
    near, kv_across, across, wq_other, far, w_out_now, done = together(
        (near, kv_across, across, wq_other, far, w_out_now, done)
    )
    chunk = {0: u, 2: across, 4: near, 8: far}
    kv = plus(kv[0], kv_across)

    early, more, late = (0, 2, 4), (8, 10, 12), (6, 14)
    pay = call(
        functools.partial(query_kernel, early),
        partial,
        (me, done, gain2, w_query, wq_other) + tuple(chunk[rel] for rel in early),
        [SMEM, ANY, VMEM, HBM, HBM] + [VMEM] * len(early),
        [
            pltpu.VMEM((len(early), width, 2 * HD), bf16),
            pltpu.VMEM(gain2.shape, f32),
            dma((2 * len(early),)),
        ],
        micros=10,
    )
    wo_other = swap(w_out_now, CORE)
    chunk[12] = swap(chunk[8], NEAR)
    chunk[10] = swap(chunk[8], ACROSS)
    pay, kv = together((pay, kv))
    alike = [[4 * z + low for z in range(count // 4)] for low in range(4)]
    kv = lax.all_to_all(kv, "tensor", 0, 0, axis_index_groups=alike, tiled=True)
    done = after(chunk[12], chunk[10])
    done, chunk[2], chunk[12], chunk[10], pay, _ = together((done, chunk[2], chunk[12], chunk[10], pay, w_out_now))

    chunk[14] = swap(chunk[12], ACROSS)
    chunk[6] = swap(chunk[2], NEAR)
    pay, ahead = call(
        functools.partial(more_kernel, more, late),
        (partial, jax.ShapeDtypeStruct((len(late), width, 2 * HD), bf16)),
        (me, done, gain2, w_query, wq_other, pay) + tuple(chunk[rel] for rel in more),
        [SMEM, ANY, VMEM, HBM, HBM, VMEM] + [VMEM] * len(more),
        [
            pltpu.VMEM((len(more), width, 2 * HD), bf16),
            pltpu.VMEM(gain2.shape, f32),
            dma((2 * len(more + late),)),
        ],
        micros=20,
    )
    kv, pay = together((kv, pay))
    kv = jnp.sum(kv.astype(f32), axis=0).astype(bf16)
    kv_other = swap(kv, CORE)
    pay = call(
        functools.partial(last_kernel, late),
        partial,
        (me, after(after(chunk[14], chunk[6], micros=10), micros=10), gain2, ahead, pay) + tuple(chunk[rel] for rel in late),
        [SMEM, ANY] + [VMEM] * (3 + len(late)),
        [pltpu.VMEM(gain2.shape, f32)],
    )
    got = swap(pay, CORE)

    blen = tokens // NBLOCK
    positions = (block_order[:, None] * blen + jnp.arange(blen)[None, :]).reshape(-1)
    half = HD // 2
    freqs = 500000.0 ** (-(jnp.arange(half).astype(f32) * 2.0) / HD)
    angle = positions.astype(f32)[:, None] * freqs[None, :]
    cosine, sine = jnp.cos(angle), jnp.sin(angle)
    cosine = jnp.concatenate([cosine, cosine], axis=1)
    sine = jnp.concatenate([-sine, sine], axis=1)

    def buffers(n):
        return [pltpu.VMEM((n, HD, width), bf16), pltpu.VMEM((n, HD, width), bf16), dma((2 * n,))]

    args = (me, after(kv_other, micros=10), pay, got, kv, kv_other, cosine, sine, positions[None, :], positions[:, None], w_out, wo_other)
    att, t14a, t14b = call(
        functools.partial(attend_kernel, count * width, (14,)),
        (jax.ShapeDtypeStruct((tokens, 2 * HD), bf16), half_block, half_block),
        args,
        [SMEM, ANY] + [VMEM] * 8 + [HBM] * 2,
        buffers(1),
    )

    x14a = swap(t14a, ACROSS)
    rels = (10, 6, 2, 12, 8, 4, 0)
    t10a, t10b, t6a, t6b, t2, t12a, t12b, t8a, t8b, t4a, t4b, t0 = call(
        functools.partial(term_kernel, rels),
        (half_block,) * 4 + (block,) + (half_wide,) * 6 + (wide,),
        (me, att, w_out, wo_other),
        [SMEM, VMEM, HBM, HBM],
        buffers(len(rels)),
        micros=20,
    )
    x14b = swap(t14b, ACROSS)
    x14a, t10a = together((x14a, t10a))
    n12a = swap(plus(t12a, x14a), NEAR)
    x10a = swap(t10a, ACROSS)
    x14b, t10b, t6a, t6b = together((x14b, t10b, t6a, t6b))
    n12b = swap(plus(t12b, x14b), NEAR)
    x10b = swap(t10b, ACROSS)
    x6a = swap(t6a, ACROSS)
    n8a = swap(plus(t8a, x10a, n12a), FAR)
    n12b, x10b, t6b = together((n12b, x10b, t6b))
    x6b = swap(t6b, ACROSS)
    n8b = swap(plus(t8b, x10b, n12b), FAR)
    _, t2 = together((x6a, t2))
    x2 = swap(t2, ACROSS)
    n4a = swap(plus(t4a, x6a), NEAR)
    n4b = swap(plus(t4b, x6b), NEAR)
    parts = (t0, x2, n4a, n4b, n8a, n8b)
    return call(
        functools.partial(final_kernel, len(parts)),
        (block, jax.ShapeDtypeStruct(x_scales.shape, bf16)),
        (me, after(n8b), x_coded, x_scales, sign2) + parts,
        [SMEM, ANY] + [VMEM] * (3 + len(parts)),
    )


def per_device(*args):
    if lax.axis_size("tensor") == 16:
        return paired(*args)
    return general(*args)


def solution(mesh):
    in_specs = (
        P("group", "tensor"),
        P("tensor", "group"),
        P(),
        P("group"),
        P(),
        P(None, "tensor"),
        P("tensor", None),
        P("tensor", None),
        P("tensor", None),
    )
    out_specs = (P("group", "tensor"), P("tensor", "group"))
    return jax.shard_map(
        per_device, mesh=mesh, in_specs=in_specs, out_specs=out_specs, check_vma=False
    )
```

```python
import functools
import math

import jax
import jax.numpy as jnp
from jax import lax
from jax.experimental import pallas as pl
from jax.experimental.pallas import tpu as pltpu
from jax.sharding import PartitionSpec as P

HD = 128
KVH = 8
BLK = 128
NBLOCK = 16


HIGH = lax.Precision.HIGHEST


def hadamard(width):
    idx = jnp.arange(width)
    parity = jnp.zeros((width, width), jnp.int32)
    bit = 1
    while bit < width:
        parity = parity + idx[:, None] // bit % 2 * (idx[None, :] // bit % 2)
        bit = bit * 2
    return jnp.where(parity % 2 == 0, 1.0, -1.0).astype(jnp.float32) / jnp.sqrt(jnp.float32(width))


def rotate_rows(value, sgn, mat):
    rows = value.shape[0]
    blocks = (value * sgn).reshape(rows, -1, mat.shape[0])
    return jnp.einsum("tnb,bc->tnc", blocks, mat, precision=HIGH).reshape(rows, -1)


def unrotate_rows(value, sgn, mat):
    rows = value.shape[0]
    blocks = value.reshape(rows, -1, mat.shape[0])
    return jnp.einsum("tnb,bc->tnc", blocks, mat, precision=HIGH).reshape(rows, -1) * sgn


def rope(value, positions, heads):
    rows = value.shape[0]
    half = HD // 2
    freqs = 500000.0 ** (-(jnp.arange(half).astype(jnp.float32) * 2.0) / HD)
    angle = positions.astype(jnp.float32)[:, None] * freqs[None, :]
    cosine = jnp.cos(angle)[:, None, :]
    sine = jnp.sin(angle)[:, None, :]
    parts = value.reshape(rows, heads, HD)
    first = parts[:, :, :half]
    second = parts[:, :, half:]
    out = jnp.concatenate([first * cosine - second * sine, second * cosine + first * sine], axis=2)
    return out.reshape(rows, heads * HD)


def encode_pairs(joined, positions):
    width = KVH * HD
    keys = rope(joined[:, :width], positions, KVH)
    return jnp.concatenate([keys, joined[:, width:]], axis=1).astype(jnp.bfloat16)


def attend(query_head, key_head, value_head, allowed):
    score = jnp.einsum(
        "qd,kd->qk", query_head, key_head, preferred_element_type=jnp.float32
    ) / jnp.sqrt(jnp.float32(HD))
    score = jnp.where(allowed, score, -1e30)
    probs = jax.nn.softmax(score, axis=1).astype(jnp.bfloat16)
    return jnp.dot(probs, value_head, preferred_element_type=jnp.float32).astype(jnp.bfloat16)


def general(x_coded, x_scales, signs, block_order, norm_gain, w_query, w_key, w_value, w_out):
    count = lax.axis_size("tensor")
    index = lax.axis_index("tensor")
    mat = hadamard(BLK)
    sgn = (2 * signs - 1).astype(jnp.float32)
    coded_all, scales_all = (
        lax.all_gather(x_coded, "tensor", axis=1, tiled=True),
        lax.all_gather(x_scales, "tensor", axis=0, tiled=True),
    )
    tokens = coded_all.shape[0]
    nblocks = scales_all.shape[0]
    deq = (
        coded_all.astype(jnp.float32).reshape(tokens, nblocks, BLK)
        * scales_all.astype(jnp.float32).T[:, :, None]
    )
    resid = unrotate_rows(deq.reshape(tokens, -1), sgn, mat)
    inv = lax.rsqrt(jnp.mean(resid * resid, axis=1, keepdims=True) + 1e-05)
    normed = (resid * norm_gain.astype(jnp.float32) * inv).astype(jnp.bfloat16)
    rows = jnp.arange(tokens)
    blen = tokens // NBLOCK
    positions = block_order[rows // blen] * blen + rows % blen
    heads_here = w_query.shape[1] // HD
    query = rope(
        jnp.dot(normed, w_query, preferred_element_type=jnp.float32), positions, heads_here
    ).astype(jnp.bfloat16)
    width = w_key.shape[0]
    mine = lax.dynamic_slice_in_dim(normed, index * width, width, 1)
    joined_w = jnp.concatenate([w_key, w_value], axis=1)
    kv_part = jnp.dot(mine, joined_w, preferred_element_type=jnp.float32)
    share = lax.psum_scatter(kv_part, "tensor", scatter_dimension=0, tiled=True)
    share_rows = share.shape[0]
    share_pos = lax.dynamic_slice_in_dim(positions, index * share_rows, share_rows, 0)
    keyval = lax.all_gather(encode_pairs(share, share_pos), "tensor", axis=0, tiled=True)
    allowed = positions[None, :] <= positions[:, None]
    per_kv = heads_here * count // KVH
    head = index * heads_here + 0
    group = head // per_kv
    key_head = lax.dynamic_slice_in_dim(keyval, group * HD, HD, 1)
    value_head = lax.dynamic_slice_in_dim(keyval, KVH * HD + group * HD, HD, 1)
    outputs = attend(query, key_head, value_head, allowed)
    rotated_w = rotate_rows(w_out.astype(jnp.float32), sgn, mat)
    rotated = jnp.dot(outputs.astype(jnp.float32), rotated_w, precision=HIGH)
    blocks = rotated.reshape(tokens, nblocks, BLK)
    scale = (jnp.max(jnp.abs(blocks), axis=2) + 1e-06).astype(jnp.bfloat16)
    coded = (blocks / scale.astype(jnp.float32)[:, :, None]).astype(jnp.bfloat16)
    send_vals = coded.reshape(tokens, count, width)
    send_scale = scale.reshape(tokens, count, nblocks // count)
    got_vals, got_scale = (
        lax.all_to_all(send_vals, "tensor", split_axis=1, concat_axis=1, tiled=True),
        lax.all_to_all(send_scale, "tensor", split_axis=1, concat_axis=1, tiled=True),
    )
    back = (
        got_vals.astype(jnp.float32).reshape(tokens, count, width // BLK, BLK)
        * got_scale.astype(jnp.float32)[:, :, :, None]
    )
    summed = jnp.sum(back, axis=1).reshape(tokens, width)
    sgn_mine = lax.dynamic_slice_in_dim(sgn, index * width, width, 0)
    resid_mine = lax.dynamic_slice_in_dim(resid, index * width, width, 1)
    newres = resid_mine + unrotate_rows(summed, sgn_mine, mat)
    final = rotate_rows(newres, sgn_mine, mat).reshape(tokens, width // BLK, BLK)
    out_scale = (jnp.max(jnp.abs(final), axis=2) + 1e-06).astype(jnp.bfloat16)
    out_coded = (final / out_scale.astype(jnp.float32)[:, :, None]).astype(jnp.bfloat16)
    return (out_coded.reshape(tokens, width), out_scale.T)


def spin(rows, cols):
    i = lax.broadcasted_iota(jnp.int32, (rows, cols), 0)
    j = lax.broadcasted_iota(jnp.int32, (rows, cols), 1)
    v = i & j
    v = v ^ (v >> 4)
    v = v ^ (v >> 2)
    v = v ^ (v >> 1)
    return (1 - 2 * (v & 1)).astype(jnp.float32).astype(jnp.bfloat16)


def dot(a, b):
    return jnp.dot(a, b, preferred_element_type=jnp.float32)


VMEM = pl.BlockSpec(memory_space=pltpu.VMEM)
SMEM = pl.BlockSpec(memory_space=pltpu.SMEM)
HBM = pl.BlockSpec(memory_space=pltpu.HBM)
ANY = pl.BlockSpec(memory_space=pl.ANY)


def call(kernel, outs, args, specs, scratch=(), micros=1):
    many = isinstance(outs, tuple)
    args = [pltpu.with_memory_space_constraint(a, pltpu.HBM) if spec is HBM else a for a, spec in zip(args, specs)]
    return pl.pallas_call(
        kernel,
        out_shape=outs,
        in_specs=specs,
        out_specs=(VMEM,) * len(outs) if many else VMEM,
        scratch_shapes=scratch,
        compiler_params=pltpu.CompilerParams(vmem_limit_bytes=32 * 2**20),
        cost_estimate=pl.CostEstimate(flops=micros * 10**9, bytes_accessed=10**6, transcendentals=0),
    )(*args)


def fetch(pairs, sems):
    copies = [pltpu.make_async_copy(src, dst, sems.at[k]) for k, (src, dst) in enumerate(pairs)]
    for copy in copies:
        copy.start()
    return copies


def unrotate_kernel(
    me, x_hbm, s_ref, sign_hbm, gain_hbm, u_ref, x, sign, gain, held, sems
):
    per = sign.shape[0]
    at = pl.multiple_of(me[0] * per, per)
    copies = fetch(
        ((gain_hbm, gain), (sign_hbm.at[pl.ds(at, per), :], sign), (x_hbm, x)),
        sems,
    )

    had = spin(BLK, BLK)
    copies[0].wait()
    held[...] = gain[...].astype(jnp.float32)
    copies[1].wait()
    sg = held[pl.ds(at, per), :] * ((2 * sign[...] - 1).astype(jnp.float32) / math.sqrt(BLK))
    scale = s_ref[...].astype(jnp.float32).T
    copies[2].wait()
    tokens = x.shape[0]
    stacked = jnp.concatenate([x[:, b * BLK : (b + 1) * BLK] for b in range(per)], axis=0)
    turned = dot(stacked, had)
    for b in range(per):
        part = turned[b * tokens : (b + 1) * tokens] * scale[:, b : b + 1]
        u_ref[:, b * BLK : (b + 1) * BLK] = (part * sg[b : b + 1, :]).astype(jnp.bfloat16)


def token_kernel(*refs):
    refs[-1][...] = jnp.zeros_like(refs[-1])


def keyval_kernel(me, u_ref, wk_hbm, wv_hbm, kv_ref, first, second, sems):
    copies = fetch(((wk_hbm, first), (wv_hbm, second)), sems)
    core, chip = me[0] & 1, me[0] >> 1
    for kind, weights in enumerate((first, second)):
        copies[kind].wait()
        part = dot(u_ref[...], weights[...]).astype(jnp.bfloat16)
        for p in range(KVH):
            kv_ref[1 - (core ^ kind), (chip ^ p) & 1, p >> 1] = part[:, p * HD : (p + 1) * HD]


def joint(me, w_hbm, x_hbm, rel, into):
    width = into.shape[0]
    at = pl.ds(pl.multiple_of((me[0] ^ rel) * width, width), width)
    return [(w_hbm.at[at, :], into.at[:, pl.ds(0, HD)]), (x_hbm.at[at, :], into.at[:, pl.ds(HD, HD)])]


def products(me, rel, u, weights, held):
    per = u.shape[1] // BLK
    inverse = held[pl.ds(pl.multiple_of((me[0] ^ rel) * per, per), per), :]
    square = 0.0
    for b in range(per):
        r = u[:, b * BLK : (b + 1) * BLK].astype(jnp.float32) * inverse[b : b + 1, :]
        square = square + r * r
    return dot(u, weights), square


def query_kernel(rels, me, token, gain_ref, w_hbm, x_hbm, *refs):
    n = len(rels)
    us, (pay_ref, ws, held, sems) = refs[:n], refs[n:]
    pairs = []
    for k, rel in enumerate(rels):
        pairs += joint(me, w_hbm, x_hbm, rel, ws.at[k])
    copies = fetch(pairs, sems)
    held[...] = 1.0 / gain_ref[...].astype(jnp.float32)
    pay, square = 0.0, 0.0
    for k, rel in enumerate(rels):
        copies[2 * k].wait()
        copies[2 * k + 1].wait()
        part, squares = products(me, rel, us[k][...], ws[k], held)
        pay, square = pay + part, square + squares
    pay_ref[:, : 2 * HD] = pay
    pay_ref[:, 2 * HD :] = square


def more_kernel(rels, ahead, me, done, gain_ref, w_hbm, x_hbm, before_ref, *refs):
    n = len(rels)
    us, (pay_ref, ahead_ref, ws, held, sems) = refs[:n], refs[n:]
    pairs = []
    for k, rel in enumerate(rels):
        pairs += joint(me, w_hbm, x_hbm, rel, ws.at[k])
    for k, rel in enumerate(ahead):
        pairs += joint(me, w_hbm, x_hbm, rel, ahead_ref.at[k])
    copies = fetch(pairs, sems)
    held[...] = 1.0 / gain_ref[...].astype(jnp.float32)
    pay, square = before_ref[:, : 2 * HD], before_ref[:, 2 * HD :]
    for k, rel in enumerate(rels):
        copies[2 * k].wait()
        copies[2 * k + 1].wait()
        part, squares = products(me, rel, us[k][...], ws[k], held)
        pay, square = pay + part, square + squares
    for copy in copies[2 * n :]:
        copy.wait()
    pay_ref[:, : 2 * HD] = pay
    pay_ref[:, 2 * HD :] = square


def last_kernel(rels, me, done, gain_ref, w_ref, before_ref, *refs):
    us, (pay_ref, held) = refs[:-2], refs[-2:]
    held[...] = 1.0 / gain_ref[...].astype(jnp.float32)
    pay, square = before_ref[:, : 2 * HD], before_ref[:, 2 * HD :]
    for k, rel in enumerate(rels):
        part, squares = products(me, rel, us[k][...], w_ref[k], held)
        pay, square = pay + part, square + squares
    pay_ref[:, : 2 * HD] = pay
    pay_ref[:, 2 * HD :] = square


def turn(value, cosine, sine):
    half = HD // 2
    swapped = jnp.concatenate([value[:, half:], value[:, :half]], axis=1)
    return (value * cosine + swapped * sine).astype(jnp.bfloat16)


def columns(me, rel, width):
    return pl.ds(pl.multiple_of((me[0] ^ rel) * width, width), width)


def put(outs, value):
    at = 0
    while at < value.shape[0]:
        rows = outs[0].shape[0]
        outs[0][...] = value[at : at + rows].astype(outs[0].dtype)
        at, outs = at + rows, outs[1:]
    return outs


def attend_kernel(total, rels, me, done, pay_ref, got_ref, kv_ref, kvx_ref, cos_ref, sin_ref, row_ref, col_ref, w_hbm, x_hbm, *refs):
    att_ref, outs, (ws, xs, sems) = refs[0], refs[1:-3], refs[-3:]
    width = ws.shape[2]
    copies = fetch(
        [(src.at[:, columns(me, rel, width)], dst.at[k]) for k, rel in enumerate(rels) for src, dst in ((w_hbm, ws), (x_hbm, xs))],
        sems,
    )
    square = jnp.sum(pay_ref[:, 2 * HD :] + got_ref[:, 2 * HD :], axis=1, keepdims=True)
    inv = lax.rsqrt(square / total + 1e-05)
    cosine, sine = cos_ref[...], sin_ref[...]
    core = me[0] & 1
    mine, theirs = kv_ref[...].astype(jnp.float32), kvx_ref[...].astype(jnp.float32)
    key = turn(jnp.where(core == 0, mine, theirs) * inv, cosine, sine)
    value = (jnp.where(core == 0, theirs, mine) * inv).astype(jnp.bfloat16)
    allowed = row_ref[...] <= col_ref[...]
    heads = []
    for at in range(2):
        query = pay_ref[:, at * HD : (at + 1) * HD] + got_ref[:, (1 - at) * HD : (2 - at) * HD]
        query = turn(query * inv, cosine, sine)
        score = lax.dot_general(query, key, (((1,), (1,)), ((), ())), preferred_element_type=jnp.float32)
        score = jnp.where(allowed, score / math.sqrt(HD), -1e30)
        weight = jnp.exp(score - jnp.max(score, axis=1, keepdims=True))
        probs = (weight / jnp.sum(weight, axis=1, keepdims=True)).astype(jnp.bfloat16)
        head = dot(probs, value).astype(jnp.bfloat16)
        att_ref[:, at * HD : (at + 1) * HD] = head
        heads.append(head)
    for k in range(len(rels)):
        copies[2 * k].wait()
        copies[2 * k + 1].wait()
        outs = put(outs, dot(heads[0], ws[k]) + dot(heads[1], xs[k]))


def term_kernel(rels, me, att_ref, w_hbm, x_hbm, *refs):
    outs, (ws, xs, sems) = refs[:-3], refs[-3:]
    width = ws.shape[2]
    copies = fetch(
        [(src.at[:, columns(me, rel, width)], dst.at[k]) for k, rel in enumerate(rels) for src, dst in ((w_hbm, ws), (x_hbm, xs))],
        sems,
    )
    for k in range(len(rels)):
        copies[2 * k].wait()
        copies[2 * k + 1].wait()
        outs = put(outs, dot(att_ref[:, :HD], ws[k]) + dot(att_ref[:, HD:], xs[k]))


def final_kernel(n, me, done, x_ref, s_ref, sign_ref, *refs):
    had = spin(BLK, BLK)
    scale = s_ref[...].astype(jnp.float32).T
    per = s_ref.shape[0]
    sign = (2 * sign_ref[pl.ds(pl.multiple_of(me[0] * per, per), per), :] - 1).astype(jnp.float32) / math.sqrt(BLK)
    parts, (coded_ref, scales_ref) = refs[:n], refs[n:]
    tokens = x_ref.shape[0]

    def piece(at):
        held, total = [], 0.0
        for ref in parts:
            held.append(ref[:, at].astype(jnp.float32))
            if sum(h.shape[0] for h in held) == tokens:
                total, held = total + jnp.concatenate(held, axis=0), []
        return total

    sums = jnp.concatenate([piece(slice(b * BLK, (b + 1) * BLK)) * sign[b : b + 1, :] for b in range(per)], axis=0)
    high = sums.astype(jnp.bfloat16)
    rest = sums - high.astype(jnp.float32)
    mid = rest.astype(jnp.bfloat16)
    low = (rest - mid.astype(jnp.float32)).astype(jnp.bfloat16)
    turned = dot(high, had) + (dot(mid, had) + dot(low, had))
    tops = []
    for b in range(per):
        at = slice(b * BLK, (b + 1) * BLK)
        new = turned[b * tokens : (b + 1) * tokens] + x_ref[:, at].astype(jnp.float32) * scale[:, b : b + 1]
        top = (jnp.max(jnp.abs(new), axis=1, keepdims=True) + 1e-06).astype(jnp.bfloat16).astype(jnp.float32)
        coded_ref[:, at] = (new / top).astype(jnp.bfloat16)
        tops.append(top)
    scales_ref[...] = jnp.concatenate(tops, axis=1).T.astype(jnp.bfloat16)


def swap(value, rel):
    count = lax.axis_size("tensor")
    return lax.ppermute(value, "tensor", [(i, i ^ rel) for i in range(count)])


CORE, ACROSS, NEAR, FAR = 1, 2, 4, 8


def paired(x_coded, x_scales, signs, block_order, norm_gain, w_query, w_key, w_value, w_out):
    count = lax.axis_size("tensor")
    index = lax.axis_index("tensor")
    me = jnp.reshape(index, (1,)).astype(jnp.int32)
    tokens, width = x_coded.shape
    bf16, f32 = jnp.bfloat16, jnp.float32
    block = jax.ShapeDtypeStruct((tokens, width), bf16)
    wide = jax.ShapeDtypeStruct((tokens, width), f32)
    half_block = jax.ShapeDtypeStruct((tokens // 2, width), bf16)
    half_wide = jax.ShapeDtypeStruct((tokens // 2, width), f32)
    partial = jax.ShapeDtypeStruct((tokens, 3 * HD), f32)
    dma = pltpu.SemaphoreType.DMA
    together = lax.optimization_barrier
    sign2 = signs.reshape(-1, BLK)
    gain2 = norm_gain.reshape(-1, BLK)

    def plus(*parts):
        return sum(p.astype(f32) for p in parts).astype(bf16)

    def after(*arrays, micros=3):
        return call(token_kernel, jax.ShapeDtypeStruct((8, BLK), f32), arrays, [ANY] * len(arrays), micros=micros)

    u = call(
        unrotate_kernel,
        block,
        (me, x_coded, x_scales, sign2, gain2),
        [SMEM, HBM, VMEM, HBM, HBM],
        [
            pltpu.VMEM(x_coded.shape, bf16),
            pltpu.VMEM((width // BLK, BLK), jnp.int32),
            pltpu.VMEM(gain2.shape, bf16),
            pltpu.VMEM(gain2.shape, f32),
            dma((3,)),
        ],
    )

    _, w_query_now = together((u, w_query))
    wq_other = swap(w_query_now, CORE)
    kv = call(
        keyval_kernel,
        jax.ShapeDtypeStruct((2, 2, KVH // 2, tokens, HD), bf16),
        (me, u, w_key, w_value),
        [SMEM, VMEM, HBM, HBM],
        [pltpu.VMEM(w_key.shape, bf16), pltpu.VMEM(w_key.shape, bf16), dma((2,))],
        micros=20,
    )
    kv = plus(kv[1], swap(kv[0], CORE))
    kv_across = swap(kv[1], ACROSS)
    far = swap(u, FAR)
    across = swap(u, ACROSS)
    near = swap(u, NEAR)
    w_out_now = w_out
    done = after(after(across, near, micros=10), far, micros=30)
    near, kv_across, across, wq_other, far, w_out_now, done = together(
        (near, kv_across, across, wq_other, far, w_out_now, done)
    )
    chunk = {0: u, 2: across, 4: near, 8: far}
    kv = plus(kv[0], kv_across)

    early, more, late = (0, 2, 4), (8, 10, 12), (6, 14)
    pay = call(
        functools.partial(query_kernel, early),
        partial,
        (me, done, gain2, w_query, wq_other) + tuple(chunk[rel] for rel in early),
        [SMEM, ANY, VMEM, HBM, HBM] + [VMEM] * len(early),
        [
            pltpu.VMEM((len(early), width, 2 * HD), bf16),
            pltpu.VMEM(gain2.shape, f32),
            dma((2 * len(early),)),
        ],
        micros=10,
    )
    wo_other = swap(w_out_now, CORE)
    chunk[12] = swap(chunk[8], NEAR)
    chunk[10] = swap(chunk[8], ACROSS)
    pay, kv = together((pay, kv))
    alike = [[4 * z + low for z in range(count // 4)] for low in range(4)]
    kv = lax.all_to_all(kv, "tensor", 0, 0, axis_index_groups=alike, tiled=True)
    done = after(chunk[12], chunk[10])
    done, chunk[2], chunk[12], chunk[10], pay, _ = together((done, chunk[2], chunk[12], chunk[10], pay, w_out_now))

    chunk[14] = swap(chunk[12], ACROSS)
    chunk[6] = swap(chunk[2], NEAR)
    pay, ahead = call(
        functools.partial(more_kernel, more, late),
        (partial, jax.ShapeDtypeStruct((len(late), width, 2 * HD), bf16)),
        (me, done, gain2, w_query, wq_other, pay) + tuple(chunk[rel] for rel in more),
        [SMEM, ANY, VMEM, HBM, HBM, VMEM] + [VMEM] * len(more),
        [
            pltpu.VMEM((len(more), width, 2 * HD), bf16),
            pltpu.VMEM(gain2.shape, f32),
            dma((2 * len(more + late),)),
        ],
        micros=20,
    )
    kv, pay = together((kv, pay))
    kv = jnp.sum(kv.astype(f32), axis=0).astype(bf16)
    kv_other = swap(kv, CORE)
    pay = call(
        functools.partial(last_kernel, late),
        partial,
        (me, after(after(chunk[14], chunk[6], micros=10), micros=10), gain2, ahead, pay) + tuple(chunk[rel] for rel in late),
        [SMEM, ANY] + [VMEM] * (3 + len(late)),
        [pltpu.VMEM(gain2.shape, f32)],
    )
    got = swap(pay, CORE)

    blen = tokens // NBLOCK
    positions = (block_order[:, None] * blen + jnp.arange(blen)[None, :]).reshape(-1)
    half = HD // 2
    freqs = 500000.0 ** (-(jnp.arange(half).astype(f32) * 2.0) / HD)
    angle = positions.astype(f32)[:, None] * freqs[None, :]
    cosine, sine = jnp.cos(angle), jnp.sin(angle)
    cosine = jnp.concatenate([cosine, cosine], axis=1)
    sine = jnp.concatenate([-sine, sine], axis=1)

    def buffers(n):
        return [pltpu.VMEM((n, HD, width), bf16), pltpu.VMEM((n, HD, width), bf16), dma((2 * n,))]

    args = (me, after(kv_other, micros=10), pay, got, kv, kv_other, cosine, sine, positions[None, :], positions[:, None], w_out, wo_other)
    att, t14a, t14b = call(
        functools.partial(attend_kernel, count * width, (14,)),
        (jax.ShapeDtypeStruct((tokens, 2 * HD), bf16), half_block, half_block),
        args,
        [SMEM, ANY] + [VMEM] * 8 + [HBM] * 2,
        buffers(1),
    )

    x14a = swap(t14a, ACROSS)
    rels = (10, 6, 2, 12, 8, 4, 0)
    t10a, t10b, t6a, t6b, t2, t12a, t12b, t8a, t8b, t4a, t4b, t0 = call(
        functools.partial(term_kernel, rels),
        (half_block,) * 4 + (block,) + (half_wide,) * 6 + (wide,),
        (me, att, w_out, wo_other),
        [SMEM, VMEM, HBM, HBM],
        buffers(len(rels)),
        micros=20,
    )
    x14b = swap(t14b, ACROSS)
    x14a, t10a = together((x14a, t10a))
    n12a = swap(plus(t12a, x14a), NEAR)
    x10a = swap(t10a, ACROSS)
    x14b, t10b, t6a, t6b = together((x14b, t10b, t6a, t6b))
    n12b = swap(plus(t12b, x14b), NEAR)
    x10b = swap(t10b, ACROSS)
    x6a = swap(t6a, ACROSS)
    n8a = swap(plus(t8a, x10a, n12a), FAR)
    n12b, x10b, t6b = together((n12b, x10b, t6b))
    x6b = swap(t6b, ACROSS)
    n8b = swap(plus(t8b, x10b, n12b), FAR)
    _, t2 = together((x6a, t2))
    x2 = swap(t2, ACROSS)
    n4a = swap(plus(t4a, x6a), NEAR)
    n4b = swap(plus(t4b, x6b), NEAR)
    parts = (t0, x2, n4a, n4b, n8a, n8b)
    return call(
        functools.partial(final_kernel, len(parts)),
        (block, jax.ShapeDtypeStruct(x_scales.shape, bf16)),
        (me, after(n8b), x_coded, x_scales, sign2) + parts,
        [SMEM, ANY] + [VMEM] * (3 + len(parts)),
    )


def per_device(*args):
    if lax.axis_size("tensor") == 16:
        return paired(*args)
    return general(*args)


def solution(mesh):
    in_specs = (
        P("group", "tensor"),
        P("tensor", "group"),
        P(),
        P("group"),
        P(),
        P(None, "tensor"),
        P("tensor", None),
        P("tensor", None),
        P("tensor", None),
    )
    out_specs = (P("group", "tensor"), P("tensor", "group"))
    return jax.shard_map(
        per_device, mesh=mesh, in_specs=in_specs, out_specs=out_specs, check_vma=False
    )
```

```python
import functools
import math

import jax
import jax.numpy as jnp
from jax import lax
from jax.experimental import pallas as pl
from jax.experimental.pallas import tpu as pltpu
from jax.sharding import PartitionSpec as P

HD = 128
KVH = 8
BLK = 128
NBLOCK = 16


HIGH = lax.Precision.HIGHEST


def hadamard(width):
    idx = jnp.arange(width)
    parity = jnp.zeros((width, width), jnp.int32)
    bit = 1
    while bit < width:
        parity = parity + idx[:, None] // bit % 2 * (idx[None, :] // bit % 2)
        bit = bit * 2
    return jnp.where(parity % 2 == 0, 1.0, -1.0).astype(jnp.float32) / jnp.sqrt(jnp.float32(width))


def rotate_rows(value, sgn, mat):
    rows = value.shape[0]
    blocks = (value * sgn).reshape(rows, -1, mat.shape[0])
    return jnp.einsum("tnb,bc->tnc", blocks, mat, precision=HIGH).reshape(rows, -1)


def unrotate_rows(value, sgn, mat):
    rows = value.shape[0]
    blocks = value.reshape(rows, -1, mat.shape[0])
    return jnp.einsum("tnb,bc->tnc", blocks, mat, precision=HIGH).reshape(rows, -1) * sgn


def rope(value, positions, heads):
    rows = value.shape[0]
    half = HD // 2
    freqs = 500000.0 ** (-(jnp.arange(half).astype(jnp.float32) * 2.0) / HD)
    angle = positions.astype(jnp.float32)[:, None] * freqs[None, :]
    cosine = jnp.cos(angle)[:, None, :]
    sine = jnp.sin(angle)[:, None, :]
    parts = value.reshape(rows, heads, HD)
    first = parts[:, :, :half]
    second = parts[:, :, half:]
    out = jnp.concatenate([first * cosine - second * sine, second * cosine + first * sine], axis=2)
    return out.reshape(rows, heads * HD)


def encode_pairs(joined, positions):
    width = KVH * HD
    keys = rope(joined[:, :width], positions, KVH)
    return jnp.concatenate([keys, joined[:, width:]], axis=1).astype(jnp.bfloat16)


def attend(query_head, key_head, value_head, allowed):
    score = jnp.einsum(
        "qd,kd->qk", query_head, key_head, preferred_element_type=jnp.float32
    ) / jnp.sqrt(jnp.float32(HD))
    score = jnp.where(allowed, score, -1e30)
    probs = jax.nn.softmax(score, axis=1).astype(jnp.bfloat16)
    return jnp.dot(probs, value_head, preferred_element_type=jnp.float32).astype(jnp.bfloat16)


def general(x_coded, x_scales, signs, block_order, norm_gain, w_query, w_key, w_value, w_out):
    count = lax.axis_size("tensor")
    index = lax.axis_index("tensor")
    mat = hadamard(BLK)
    sgn = (2 * signs - 1).astype(jnp.float32)
    coded_all, scales_all = (
        lax.all_gather(x_coded, "tensor", axis=1, tiled=True),
        lax.all_gather(x_scales, "tensor", axis=0, tiled=True),
    )
    tokens = coded_all.shape[0]
    nblocks = scales_all.shape[0]
    deq = (
        coded_all.astype(jnp.float32).reshape(tokens, nblocks, BLK)
        * scales_all.astype(jnp.float32).T[:, :, None]
    )
    resid = unrotate_rows(deq.reshape(tokens, -1), sgn, mat)
    inv = lax.rsqrt(jnp.mean(resid * resid, axis=1, keepdims=True) + 1e-05)
    normed = (resid * norm_gain.astype(jnp.float32) * inv).astype(jnp.bfloat16)
    rows = jnp.arange(tokens)
    blen = tokens // NBLOCK
    positions = block_order[rows // blen] * blen + rows % blen
    heads_here = w_query.shape[1] // HD
    query = rope(
        jnp.dot(normed, w_query, preferred_element_type=jnp.float32), positions, heads_here
    ).astype(jnp.bfloat16)
    width = w_key.shape[0]
    mine = lax.dynamic_slice_in_dim(normed, index * width, width, 1)
    joined_w = jnp.concatenate([w_key, w_value], axis=1)
    kv_part = jnp.dot(mine, joined_w, preferred_element_type=jnp.float32)
    share = lax.psum_scatter(kv_part, "tensor", scatter_dimension=0, tiled=True)
    share_rows = share.shape[0]
    share_pos = lax.dynamic_slice_in_dim(positions, index * share_rows, share_rows, 0)
    keyval = lax.all_gather(encode_pairs(share, share_pos), "tensor", axis=0, tiled=True)
    allowed = positions[None, :] <= positions[:, None]
    per_kv = heads_here * count // KVH
    head = index * heads_here + 0
    group = head // per_kv
    key_head = lax.dynamic_slice_in_dim(keyval, group * HD, HD, 1)
    value_head = lax.dynamic_slice_in_dim(keyval, KVH * HD + group * HD, HD, 1)
    outputs = attend(query, key_head, value_head, allowed)
    rotated_w = rotate_rows(w_out.astype(jnp.float32), sgn, mat)
    rotated = jnp.dot(outputs.astype(jnp.float32), rotated_w, precision=HIGH)
    blocks = rotated.reshape(tokens, nblocks, BLK)
    scale = (jnp.max(jnp.abs(blocks), axis=2) + 1e-06).astype(jnp.bfloat16)
    coded = (blocks / scale.astype(jnp.float32)[:, :, None]).astype(jnp.bfloat16)
    send_vals = coded.reshape(tokens, count, width)
    send_scale = scale.reshape(tokens, count, nblocks // count)
    got_vals, got_scale = (
        lax.all_to_all(send_vals, "tensor", split_axis=1, concat_axis=1, tiled=True),
        lax.all_to_all(send_scale, "tensor", split_axis=1, concat_axis=1, tiled=True),
    )
    back = (
        got_vals.astype(jnp.float32).reshape(tokens, count, width // BLK, BLK)
        * got_scale.astype(jnp.float32)[:, :, :, None]
    )
    summed = jnp.sum(back, axis=1).reshape(tokens, width)
    sgn_mine = lax.dynamic_slice_in_dim(sgn, index * width, width, 0)
    resid_mine = lax.dynamic_slice_in_dim(resid, index * width, width, 1)
    newres = resid_mine + unrotate_rows(summed, sgn_mine, mat)
    final = rotate_rows(newres, sgn_mine, mat).reshape(tokens, width // BLK, BLK)
    out_scale = (jnp.max(jnp.abs(final), axis=2) + 1e-06).astype(jnp.bfloat16)
    out_coded = (final / out_scale.astype(jnp.float32)[:, :, None]).astype(jnp.bfloat16)
    return (out_coded.reshape(tokens, width), out_scale.T)


def spin(rows, cols):
    i = lax.broadcasted_iota(jnp.int32, (rows, cols), 0)
    j = lax.broadcasted_iota(jnp.int32, (rows, cols), 1)
    v = i & j
    v = v ^ (v >> 4)
    v = v ^ (v >> 2)
    v = v ^ (v >> 1)
    return (1 - 2 * (v & 1)).astype(jnp.float32).astype(jnp.bfloat16)


def dot(a, b):
    return jnp.dot(a, b, preferred_element_type=jnp.float32)


VMEM = pl.BlockSpec(memory_space=pltpu.VMEM)
SMEM = pl.BlockSpec(memory_space=pltpu.SMEM)
HBM = pl.BlockSpec(memory_space=pltpu.HBM)
ANY = pl.BlockSpec(memory_space=pl.ANY)


def call(kernel, outs, args, specs, scratch=(), micros=1):
    many = isinstance(outs, tuple)
    args = [pltpu.with_memory_space_constraint(a, pltpu.HBM) if spec is HBM else a for a, spec in zip(args, specs)]
    return pl.pallas_call(
        kernel,
        out_shape=outs,
        in_specs=specs,
        out_specs=(VMEM,) * len(outs) if many else VMEM,
        scratch_shapes=scratch,
        compiler_params=pltpu.CompilerParams(vmem_limit_bytes=32 * 2**20),
        cost_estimate=pl.CostEstimate(flops=micros * 10**9, bytes_accessed=10**6, transcendentals=0),
    )(*args)


def fetch(pairs, sems):
    copies = [pltpu.make_async_copy(src, dst, sems.at[k]) for k, (src, dst) in enumerate(pairs)]
    for copy in copies:
        copy.start()
    return copies


def unrotate_kernel(
    me, x_hbm, s_hbm, sign_hbm, gain_hbm, u_ref, x, s, sign, gain, held, sems
):
    per = sign.shape[0]
    at = pl.multiple_of(me[0] * per, per)
    copies = fetch(
        ((gain_hbm, gain), (sign_hbm.at[pl.ds(at, per), :], sign), (s_hbm, s), (x_hbm, x)),
        sems,
    )

    had = spin(BLK, BLK)
    copies[0].wait()
    held[...] = gain[...].astype(jnp.float32)
    copies[1].wait()
    sg = held[pl.ds(at, per), :] * ((2 * sign[...] - 1).astype(jnp.float32) / math.sqrt(BLK))
    copies[2].wait()
    scale = s[...].astype(jnp.float32).T
    copies[3].wait()
    tokens = x.shape[0]
    stacked = jnp.concatenate([x[:, b * BLK : (b + 1) * BLK] for b in range(per)], axis=0)
    turned = dot(stacked, had)
    for b in range(per):
        part = turned[b * tokens : (b + 1) * tokens] * scale[:, b : b + 1]
        u_ref[:, b * BLK : (b + 1) * BLK] = (part * sg[b : b + 1, :]).astype(jnp.bfloat16)


def token_kernel(*refs):
    refs[-1][...] = jnp.zeros_like(refs[-1])


def keyval_kernel(me, u_ref, wk_hbm, wv_hbm, kv_ref, first, second, sems):
    copies = fetch(((wk_hbm, first), (wv_hbm, second)), sems)
    core, chip = me[0] & 1, me[0] >> 1
    for kind, weights in enumerate((first, second)):
        copies[kind].wait()
        part = dot(u_ref[...], weights[...]).astype(jnp.bfloat16)
        for p in range(KVH):
            kv_ref[1 - (core ^ kind), (chip ^ p) & 1, p >> 1] = part[:, p * HD : (p + 1) * HD]


def joint(me, w_hbm, x_hbm, rel, into):
    width = into.shape[0]
    at = pl.ds(pl.multiple_of((me[0] ^ rel) * width, width), width)
    return [(w_hbm.at[at, :], into.at[:, pl.ds(0, HD)]), (x_hbm.at[at, :], into.at[:, pl.ds(HD, HD)])]


def products(me, rel, u, weights, held):
    per = u.shape[1] // BLK
    inverse = held[pl.ds(pl.multiple_of((me[0] ^ rel) * per, per), per), :]
    square = 0.0
    for b in range(per):
        r = u[:, b * BLK : (b + 1) * BLK].astype(jnp.float32) * inverse[b : b + 1, :]
        square = square + r * r
    return dot(u, weights), square


def query_kernel(rels, me, token, gain_ref, w_hbm, x_hbm, *refs):
    n = len(rels)
    us, (pay_ref, ws, held, sems) = refs[:n], refs[n:]
    pairs = []
    for k, rel in enumerate(rels):
        pairs += joint(me, w_hbm, x_hbm, rel, ws.at[k])
    copies = fetch(pairs, sems)
    held[...] = 1.0 / gain_ref[...].astype(jnp.float32)
    pay, square = 0.0, 0.0
    for k, rel in enumerate(rels):
        copies[2 * k].wait()
        copies[2 * k + 1].wait()
        part, squares = products(me, rel, us[k][...], ws[k], held)
        pay, square = pay + part, square + squares
    pay_ref[:, : 2 * HD] = pay
    pay_ref[:, 2 * HD :] = square


def more_kernel(rels, ahead, me, done, gain_ref, w_hbm, x_hbm, before_ref, *refs):
    n = len(rels)
    us, (pay_ref, ahead_ref, ws, held, sems) = refs[:n], refs[n:]
    pairs = []
    for k, rel in enumerate(rels):
        pairs += joint(me, w_hbm, x_hbm, rel, ws.at[k])
    for k, rel in enumerate(ahead):
        pairs += joint(me, w_hbm, x_hbm, rel, ahead_ref.at[k])
    copies = fetch(pairs, sems)
    held[...] = 1.0 / gain_ref[...].astype(jnp.float32)
    pay, square = before_ref[:, : 2 * HD], before_ref[:, 2 * HD :]
    for k, rel in enumerate(rels):
        copies[2 * k].wait()
        copies[2 * k + 1].wait()
        part, squares = products(me, rel, us[k][...], ws[k], held)
        pay, square = pay + part, square + squares
    for copy in copies[2 * n :]:
        copy.wait()
    pay_ref[:, : 2 * HD] = pay
    pay_ref[:, 2 * HD :] = square


def last_kernel(rels, me, done, gain_ref, w_ref, before_ref, *refs):
    us, (pay_ref, held) = refs[:-2], refs[-2:]
    held[...] = 1.0 / gain_ref[...].astype(jnp.float32)
    pay, square = before_ref[:, : 2 * HD], before_ref[:, 2 * HD :]
    for k, rel in enumerate(rels):
        part, squares = products(me, rel, us[k][...], w_ref[k], held)
        pay, square = pay + part, square + squares
    pay_ref[:, : 2 * HD] = pay
    pay_ref[:, 2 * HD :] = square


def turn(value, cosine, sine):
    half = HD // 2
    swapped = jnp.concatenate([value[:, half:], value[:, :half]], axis=1)
    return (value * cosine + swapped * sine).astype(jnp.bfloat16)


def columns(me, rel, width):
    return pl.ds(pl.multiple_of((me[0] ^ rel) * width, width), width)


def put(outs, value):
    at = 0
    while at < value.shape[0]:
        rows = outs[0].shape[0]
        outs[0][...] = value[at : at + rows].astype(outs[0].dtype)
        at, outs = at + rows, outs[1:]
    return outs


def attend_kernel(total, rels, me, done, pay_ref, got_ref, kv_ref, kvx_ref, cos_ref, sin_ref, row_ref, col_ref, w_hbm, x_hbm, *refs):
    att_ref, outs, (ws, xs, sems) = refs[0], refs[1:-3], refs[-3:]
    width = ws.shape[2]
    copies = fetch(
        [(src.at[:, columns(me, rel, width)], dst.at[k]) for k, rel in enumerate(rels) for src, dst in ((w_hbm, ws), (x_hbm, xs))],
        sems,
    )
    square = jnp.sum(pay_ref[:, 2 * HD :] + got_ref[:, 2 * HD :], axis=1, keepdims=True)
    inv = lax.rsqrt(square / total + 1e-05)
    cosine, sine = cos_ref[...], sin_ref[...]
    core = me[0] & 1
    mine, theirs = kv_ref[...].astype(jnp.float32), kvx_ref[...].astype(jnp.float32)
    key = turn(jnp.where(core == 0, mine, theirs) * inv, cosine, sine)
    value = (jnp.where(core == 0, theirs, mine) * inv).astype(jnp.bfloat16)
    allowed = row_ref[...] <= col_ref[...]
    heads = []
    for at in range(2):
        query = pay_ref[:, at * HD : (at + 1) * HD] + got_ref[:, (1 - at) * HD : (2 - at) * HD]
        query = turn(query * inv, cosine, sine)
        score = lax.dot_general(query, key, (((1,), (1,)), ((), ())), preferred_element_type=jnp.float32)
        score = jnp.where(allowed, score / math.sqrt(HD), -1e30)
        weight = jnp.exp(score - jnp.max(score, axis=1, keepdims=True))
        probs = (weight / jnp.sum(weight, axis=1, keepdims=True)).astype(jnp.bfloat16)
        head = dot(probs, value).astype(jnp.bfloat16)
        att_ref[:, at * HD : (at + 1) * HD] = head
        heads.append(head)
    for k in range(len(rels)):
        copies[2 * k].wait()
        copies[2 * k + 1].wait()
        outs = put(outs, dot(heads[0], ws[k]) + dot(heads[1], xs[k]))


def term_kernel(rels, me, att_ref, w_hbm, x_hbm, *refs):
    outs, (ws, xs, sems) = refs[:-3], refs[-3:]
    width = ws.shape[2]
    copies = fetch(
        [(src.at[:, columns(me, rel, width)], dst.at[k]) for k, rel in enumerate(rels) for src, dst in ((w_hbm, ws), (x_hbm, xs))],
        sems,
    )
    for k in range(len(rels)):
        copies[2 * k].wait()
        copies[2 * k + 1].wait()
        outs = put(outs, dot(att_ref[:, :HD], ws[k]) + dot(att_ref[:, HD:], xs[k]))


def final_kernel(n, me, done, x_ref, s_ref, sign_ref, *refs):
    had = spin(BLK, BLK)
    scale = s_ref[...].astype(jnp.float32).T
    per = s_ref.shape[0]
    sign = (2 * sign_ref[pl.ds(pl.multiple_of(me[0] * per, per), per), :] - 1).astype(jnp.float32) / math.sqrt(BLK)
    parts, (coded_ref, scales_ref) = refs[:n], refs[n:]
    tokens = x_ref.shape[0]

    def piece(at):
        held, total = [], 0.0
        for ref in parts:
            held.append(ref[:, at].astype(jnp.float32))
            if sum(h.shape[0] for h in held) == tokens:
                total, held = total + jnp.concatenate(held, axis=0), []
        return total

    sums = jnp.concatenate([piece(slice(b * BLK, (b + 1) * BLK)) * sign[b : b + 1, :] for b in range(per)], axis=0)
    high = sums.astype(jnp.bfloat16)
    rest = sums - high.astype(jnp.float32)
    mid = rest.astype(jnp.bfloat16)
    low = (rest - mid.astype(jnp.float32)).astype(jnp.bfloat16)
    turned = dot(high, had) + (dot(mid, had) + dot(low, had))
    tops = []
    for b in range(per):
        at = slice(b * BLK, (b + 1) * BLK)
        new = turned[b * tokens : (b + 1) * tokens] + x_ref[:, at].astype(jnp.float32) * scale[:, b : b + 1]
        top = (jnp.max(jnp.abs(new), axis=1, keepdims=True) + 1e-06).astype(jnp.bfloat16).astype(jnp.float32)
        coded_ref[:, at] = (new / top).astype(jnp.bfloat16)
        tops.append(top)
    scales_ref[...] = jnp.concatenate(tops, axis=1).T.astype(jnp.bfloat16)


def swap(value, rel):
    count = lax.axis_size("tensor")
    return lax.ppermute(value, "tensor", [(i, i ^ rel) for i in range(count)])


CORE, ACROSS, NEAR, FAR = 1, 2, 4, 8


def paired(x_coded, x_scales, signs, block_order, norm_gain, w_query, w_key, w_value, w_out):
    count = lax.axis_size("tensor")
    index = lax.axis_index("tensor")
    me = jnp.reshape(index, (1,)).astype(jnp.int32)
    tokens, width = x_coded.shape
    bf16, f32 = jnp.bfloat16, jnp.float32
    block = jax.ShapeDtypeStruct((tokens, width), bf16)
    wide = jax.ShapeDtypeStruct((tokens, width), f32)
    half_block = jax.ShapeDtypeStruct((tokens // 2, width), bf16)
    half_wide = jax.ShapeDtypeStruct((tokens // 2, width), f32)
    partial = jax.ShapeDtypeStruct((tokens, 3 * HD), f32)
    dma = pltpu.SemaphoreType.DMA
    together = lax.optimization_barrier
    sign2 = signs.reshape(-1, BLK)
    gain2 = norm_gain.reshape(-1, BLK)

    def plus(*parts):
        return sum(p.astype(f32) for p in parts).astype(bf16)

    def after(*arrays, micros=3):
        return call(token_kernel, jax.ShapeDtypeStruct((8, BLK), f32), arrays, [ANY] * len(arrays), micros=micros)

    u = call(
        unrotate_kernel,
        block,
        (me, x_coded, x_scales, sign2, gain2),
        [SMEM] + [HBM] * 4,
        [
            pltpu.VMEM(x_coded.shape, bf16),
            pltpu.VMEM(x_scales.shape, bf16),
            pltpu.VMEM((width // BLK, BLK), jnp.int32),
            pltpu.VMEM(gain2.shape, bf16),
            pltpu.VMEM(gain2.shape, f32),
            dma((4,)),
        ],
    )

    _, w_query_now = together((u, w_query))
    wq_other = swap(w_query_now, CORE)
    far = swap(u, FAR)
    kv = call(
        keyval_kernel,
        jax.ShapeDtypeStruct((2, 2, KVH // 2, tokens, HD), bf16),
        (me, u, w_key, w_value),
        [SMEM, VMEM, HBM, HBM],
        [pltpu.VMEM(w_key.shape, bf16), pltpu.VMEM(w_key.shape, bf16), dma((2,))],
        micros=20,
    )
    kv = plus(kv[1], swap(kv[0], CORE))
    kv_across = swap(kv[1], ACROSS)
    across = swap(u, ACROSS)
    near = swap(u, NEAR)
    w_out_now = w_out
    done = after(after(far, across, near, micros=30), micros=10)
    across, wq_other, near, done, far, w_out_now, kv_across = together(
        (across, wq_other, near, done, far, w_out_now, kv_across)
    )
    chunk = {0: u, 2: across, 4: near, 8: far}
    kv = plus(kv[0], kv_across)

    early, more, late = (0, 2, 4), (8, 10, 12), (6, 14)
    pay = call(
        functools.partial(query_kernel, early),
        partial,
        (me, done, gain2, w_query, wq_other) + tuple(chunk[rel] for rel in early),
        [SMEM, ANY, VMEM, HBM, HBM] + [VMEM] * len(early),
        [
            pltpu.VMEM((len(early), width, 2 * HD), bf16),
            pltpu.VMEM(gain2.shape, f32),
            dma((2 * len(early),)),
        ],
        micros=20,
    )
    wo_other = swap(w_out_now, CORE)
    chunk[12] = swap(chunk[8], NEAR)
    chunk[10] = swap(chunk[8], ACROSS)
    kv, pay = together((kv, pay))
    alike = [[4 * z + low for z in range(count // 4)] for low in range(4)]
    kv = lax.all_to_all(kv, "tensor", 0, 0, axis_index_groups=alike, tiled=True)
    done = after(after(chunk[12]), chunk[10])
    done, chunk[2], chunk[12], chunk[10], pay, _ = together((done, chunk[2], chunk[12], chunk[10], pay, w_out_now))

    chunk[14] = swap(chunk[12], ACROSS)
    chunk[6] = swap(chunk[2], NEAR)
    pay, ahead = call(
        functools.partial(more_kernel, more, late),
        (partial, jax.ShapeDtypeStruct((len(late), width, 2 * HD), bf16)),
        (me, done, gain2, w_query, wq_other, pay) + tuple(chunk[rel] for rel in more),
        [SMEM, ANY, VMEM, HBM, HBM, VMEM] + [VMEM] * len(more),
        [
            pltpu.VMEM((len(more), width, 2 * HD), bf16),
            pltpu.VMEM(gain2.shape, f32),
            dma((2 * len(more + late),)),
        ],
        micros=20,
    )
    kv, pay = together((kv, pay))
    kv = jnp.sum(kv.astype(f32), axis=0).astype(bf16)
    kv_other = swap(kv, CORE)
    pay = call(
        functools.partial(last_kernel, late),
        partial,
        (me, after(after(chunk[14], chunk[6], micros=10), micros=10), gain2, ahead, pay) + tuple(chunk[rel] for rel in late),
        [SMEM, ANY] + [VMEM] * (3 + len(late)),
        [pltpu.VMEM(gain2.shape, f32)],
    )
    got = swap(pay, CORE)

    blen = tokens // NBLOCK
    positions = (block_order[:, None] * blen + jnp.arange(blen)[None, :]).reshape(-1)
    half = HD // 2
    freqs = 500000.0 ** (-(jnp.arange(half).astype(f32) * 2.0) / HD)
    angle = positions.astype(f32)[:, None] * freqs[None, :]
    cosine, sine = jnp.cos(angle), jnp.sin(angle)
    cosine = jnp.concatenate([cosine, cosine], axis=1)
    sine = jnp.concatenate([-sine, sine], axis=1)

    def buffers(n):
        return [pltpu.VMEM((n, HD, width), bf16), pltpu.VMEM((n, HD, width), bf16), dma((2 * n,))]

    args = (me, after(kv_other, micros=10), pay, got, kv, kv_other, cosine, sine, positions[None, :], positions[:, None], w_out, wo_other)
    att, t14a, t14b = call(
        functools.partial(attend_kernel, count * width, (14,)),
        (jax.ShapeDtypeStruct((tokens, 2 * HD), bf16), half_block, half_block),
        args,
        [SMEM, ANY] + [VMEM] * 8 + [HBM] * 2,
        buffers(1),
    )

    x14a = swap(t14a, ACROSS)
    rels = (10, 6, 2, 12, 8, 4, 0)
    t10a, t10b, t6a, t6b, t2, t12a, t12b, t8a, t8b, t4a, t4b, t0 = call(
        functools.partial(term_kernel, rels),
        (half_block,) * 4 + (block,) + (half_wide,) * 6 + (wide,),
        (me, att, w_out, wo_other),
        [SMEM, VMEM, HBM, HBM],
        buffers(len(rels)),
        micros=20,
    )
    x14b = swap(t14b, ACROSS)
    x14a, t10a = together((x14a, t10a))
    n12a = swap(plus(t12a, x14a), NEAR)
    x10a = swap(t10a, ACROSS)
    x14b, t10b, t6a, t6b = together((x14b, t10b, t6a, t6b))
    n12b = swap(plus(t12b, x14b), NEAR)
    x10b = swap(t10b, ACROSS)
    x6a = swap(t6a, ACROSS)
    n8a = swap(plus(t8a, x10a, n12a), FAR)
    n12b, x10b, t6b = together((n12b, x10b, t6b))
    x6b = swap(t6b, ACROSS)
    n8b = swap(plus(t8b, x10b, n12b), FAR)
    _, t2 = together((x6a, t2))
    x2 = swap(t2, ACROSS)
    n4a = swap(plus(t4a, x6a), NEAR)
    n4b = swap(plus(t4b, x6b), NEAR)
    parts = (t0, x2, n4a, n4b, n8a, n8b)
    return call(
        functools.partial(final_kernel, len(parts)),
        (block, jax.ShapeDtypeStruct(x_scales.shape, bf16)),
        (me, after(n8b), x_coded, x_scales, sign2) + parts,
        [SMEM, ANY] + [VMEM] * (3 + len(parts)),
    )


def per_device(*args):
    if lax.axis_size("tensor") == 16:
        return paired(*args)
    return general(*args)


def solution(mesh):
    in_specs = (
        P("group", "tensor"),
        P("tensor", "group"),
        P(),
        P("group"),
        P(),
        P(None, "tensor"),
        P("tensor", None),
        P("tensor", None),
        P("tensor", None),
    )
    out_specs = (P("group", "tensor"), P("tensor", "group"))
    return jax.shard_map(
        per_device, mesh=mesh, in_specs=in_specs, out_specs=out_specs, check_vma=False
    )
```
